512 devices in a mesh: row: 32 (over x, y), col: 16 (over z, core).
Axes of the slice: x: 4, y: 8, z: 8, core: 2. Of those that a mesh axis runs over, the one named last changes fastest.
Arguments:
- points: float32 [64, 16384], P(None, ('row', 'col')), may hold values from -6 to 6
- length_scales: float32 [64], replicated, may hold values from 2 to 8
- variances: float32 [2], replicated, may hold values from 0.5 to 2
- targets: float32 [16384], P(('row', 'col')), may hold values from -6 to 6
- probe_vectors: float32 [30, 16384], P(None, ('row', 'col')), may hold values from -6 to 6
Outputs:
- solves: float32 [31, 16384], P(None, ('row', 'col'))
- gradient: float32 [66], replicated
The draws below stay inside these ranges and needn't reach their ends.
All inputs are finite; a program needn't handle non-finite values.
Results may differ from the reference program's by a relative error of at most 0.0003.
Values sent between devices are 32-bit elements; how exact they have to be, the bound alone decides.
No kernel may reach another device: no remote copies, remote signals or barrier semaphores. Data moves between devices by JAX's collectives and lax.ppermute only.
A program may use at most 64 MiB of HBM per device.

```python
import math
import jax
import jax.numpy as jnp
from jax import lax

FEAT = 64
PROBES = 30
ITERS = 2
COLS = 31
POINTS = 16384


def shard_levels(stream_key, shape, shards, least, high):
    def one(dim, shards_of):
        draws = jax.random.uniform(jax.random.fold_in(jax.random.fold_in(stream_key, 6), dim), (shards_of,), jnp.float32, least / len(shards), high / len(shards))
        return jnp.repeat(jnp.exp(draws), shape[dim] // shards_of).reshape((-1,) + (1,) * (len(shape) - dim - 1))

    factor_of = one(*shards[0])
    for cut in shards[1:]:
        factor_of = factor_of * one(*cut)
    return factor_of


def scatter_about(own_key, extent, width, most, split=(), held_as=jnp.bfloat16):
    array = width * jax.random.normal(own_key, extent, jnp.float32)
    if split:
        array = array * shard_levels(own_key, extent, split, -0.22, 0.18)
    return jnp.clip(array, -most, most).astype(held_as)


def setup_inputs(seed: int = 0) -> dict:
    arg_keys = jax.random.split(jax.random.key(seed), 6)
    return {
        "points": scatter_about(arg_keys[0], (FEAT, POINTS), 1.0, 6.0, ((1, 512),), jnp.float32),
        "length_scales": jnp.clip(jnp.exp(jax.random.uniform(arg_keys[1], (FEAT,), jnp.float32, math.log(2.0), math.log(8.0))), 2.0, 8.0),
        "variances": jnp.clip(jnp.exp(jax.random.uniform(arg_keys[2], (2,), jnp.float32, math.log(0.5), math.log(2.0))), 0.5, 2.0),
        "targets": scatter_about(arg_keys[3], (POINTS,), 1.0, 6.0, ((0, 512),), jnp.float32),
        "probe_vectors": scatter_about(arg_keys[4], (PROBES, POINTS), 1.0, 6.0, ((1, 512),), jnp.float32),
    }


highest = lax.Precision.HIGHEST
root_five = 5.0 ** 0.5

def kernel_terms(left_points, right_points):
    squared = lax.optimization_barrier(jnp.sum(left_points * left_points, 0))[:, None] + lax.optimization_barrier(jnp.sum(right_points * right_points, 0))[None, :] - 2.0 * jnp.einsum('fm,fn->mn', left_points, right_points, precision=highest)
    scaled_dist = root_five * jnp.sqrt(jnp.maximum(squared, 0.0))
    decayed = jnp.exp(-scaled_dist)
    kernel_base = (1.0 + scaled_dist + scaled_dist * scaled_dist / 3.0) * decayed
    kernel_slope = 5.0 / 3.0 * (1.0 + scaled_dist) * decayed
    return (kernel_base, kernel_slope)

def gram_of(first_block, second_block):
    return jnp.einsum('cn,dn->cd', first_block, second_block, precision=highest)

def symmetric(matrix):
    return 0.5 * (matrix + matrix.T)

def solve_spd(matrix, right):
    lower = jnp.linalg.cholesky(matrix)
    return jax.scipy.linalg.cho_solve((lower, True), right)

def reference(points, length_scales, variances, targets, probe_vectors):
    total_points = points.shape[1]
    block_rows = math.gcd(total_points, 512)
    block_count = total_points // block_rows
    scaled = points / length_scales[:, None]
    rhs_block = jnp.concatenate([probe_vectors.astype(jnp.float32), targets[None, :].astype(jnp.float32)], 0)
    row_groups = scaled.reshape(FEAT, block_count, block_rows).transpose(1, 0, 2)

    def apply_kernel(values):

        def one_block(row_points):
            kernel_base, unused = kernel_terms(row_points, scaled)
            return jnp.einsum('mn,cn->cm', kernel_base, values, precision=highest)
        parts = lax.map(one_block, row_groups)
        summed = parts.transpose(1, 0, 2).reshape(COLS, total_points)
        return variances[0] * summed + variances[1] * values
    solves = jnp.zeros_like(rhs_block)
    residual = rhs_block
    direction = rhs_block
    res_gram = symmetric(gram_of(residual, residual))
    for iteration in range(ITERS):
        images = apply_kernel(direction)
        curvature = symmetric(gram_of(direction, images))
        advance = solve_spd(curvature, res_gram)
        solves = solves + jnp.einsum('cd,cn->dn', advance, direction, precision=highest)
        residual = residual - jnp.einsum('cd,cn->dn', advance, images, precision=highest)
        if iteration + 1 < ITERS:
            next_gram = symmetric(gram_of(residual, residual))
            carry_over = solve_spd(res_gram, next_gram)
            direction = residual + jnp.einsum('cd,cn->dn', carry_over, direction, precision=highest)
            res_gram = next_gram
    column_weights = jnp.concatenate([jnp.full((PROBES,), -1.0 / PROBES, jnp.float32), jnp.ones((1,), jnp.float32)])
    row_weights = solves * column_weights[:, None] * (0.5 / total_points)
    pair_block = jnp.concatenate([rhs_block[:PROBES], solves[PROBES:]], 0)
    weight_groups = row_weights.reshape(COLS, block_count, block_rows).transpose(1, 0, 2)

    def grad_block(members):
        row_points, row_left = members
        kernel_base, kernel_slope = kernel_terms(row_points, scaled)
        weight_matrix = jnp.einsum('cm,cn->mn', row_left, pair_block, precision=highest)
        weighted = weight_matrix * kernel_slope
        row_sums = lax.optimization_barrier(jnp.sum(weighted, 1))
        col_sums = lax.optimization_barrier(jnp.sum(weighted, 0))
        cross_term = jnp.einsum('mn,fn->fm', weighted, scaled, precision=highest)
        scale_terms = lax.optimization_barrier(jnp.sum(row_points * row_points * row_sums[None, :], 1)) + lax.optimization_barrier(jnp.sum(scaled * scaled * col_sums[None, :], 1)) - 2.0 * lax.optimization_barrier(jnp.sum(row_points * cross_term, 1))
        signal_term = jnp.sum(weight_matrix * kernel_base)
        return jnp.concatenate([scale_terms, signal_term[None]])
    summed = lax.optimization_barrier(jnp.sum(lax.map(grad_block, (row_groups, weight_groups)), 0))
    noise_term = variances[1] * jnp.sum(row_weights * pair_block)
    return (solves, jnp.concatenate([variances[0] * summed, noise_term[None]]))
```

```python
import jax
import jax.numpy as jnp
from jax import lax
from jax.sharding import PartitionSpec as P

PROBES = 30
COLS = 31
FEAT = 64

highest = lax.Precision.HIGHEST
root_five = 5.0**0.5


def mul(spec, left, right):
    return jnp.einsum(spec, left, right, precision=highest, preferred_element_type=jnp.float32)


def kernel_terms(left_points, right_points):
    squared = (
        jnp.sum(left_points * left_points, 1)[:, None]
        + jnp.sum(right_points * right_points, 1)[None, :]
        - 2.0 * mul("mf,nf->mn", left_points, right_points)
    )
    scaled_dist = root_five * jnp.sqrt(jnp.maximum(squared, 0.0))
    decayed = jnp.exp(-scaled_dist)
    kernel_base = (1.0 + scaled_dist + scaled_dist * scaled_dist / 3.0) * decayed
    kernel_slope = 5.0 / 3.0 * (1.0 + scaled_dist) * decayed
    return (kernel_base, kernel_slope)


def symmetric(matrix):
    return 0.5 * (matrix + matrix.T)


def solve_spd(matrix, right):
    lower = jnp.linalg.cholesky(matrix)
    return jax.scipy.linalg.cho_solve((lower, True), right)


def gather_blocks(block, axis):
    count = lax.axis_size(axis)
    spread = jnp.broadcast_to(block[None], (count,) + block.shape)
    return lax.all_to_all(spread, axis, 0, 0, tiled=True)


def sum_blocks(block, axis):
    return jnp.sum(gather_blocks(block, axis), 0)


def lanes(*pieces):
    rows = pieces[0].shape[0]
    used = sum(p.shape[1] for p in pieces)
    return jnp.concatenate(list(pieces) + [jnp.zeros((rows, 128 - used), jnp.float32)], 1)


def square32(matrix):
    return jnp.pad(matrix, ((0, 1), (0, 1)))


def local(points, length_scales, variances, targets, probe_vectors):
    row_count = lax.axis_size("row")
    col_count = lax.axis_size("col")
    width = points.shape[1]
    total_points = width * row_count * col_count
    signal_var = variances[0]
    noise_var = variances[1]
    scaled = (points / length_scales[:, None]).T
    rhs = jnp.concatenate([probe_vectors, targets[None, :]], 0).T
    own = lanes(scaled, rhs)
    row_pack = gather_blocks(own, "col").reshape(col_count * width, 128)
    col_pack = gather_blocks(own, "row").reshape(row_count * width, 128)
    row_x, row_b = row_pack[:, :FEAT], row_pack[:, FEAT : FEAT + COLS]
    col_x, col_b = col_pack[:, :FEAT], col_pack[:, FEAT : FEAT + COLS]
    base, slope = kernel_terms(row_x, col_x)

    partial = mul("mn,nc->mc", base, col_b)
    part_curv = mul("mc,md->cd", row_b, partial)
    part_gram = mul("mc,md->cd", rhs, rhs)
    chunks = jnp.pad(partial, ((0, 0), (0, 1))).reshape(col_count, width, 32)
    grams = jnp.concatenate([square32(part_curv), square32(part_gram)], 1)
    message = jnp.concatenate(
        [chunks, jnp.broadcast_to(grams[None], (col_count, 32, 64)), jnp.zeros((col_count, 32, 32), jnp.float32)], 2
    )
    summed = jnp.sum(lax.all_to_all(message, "col", 0, 0, tiled=True), 0)
    images = signal_var * summed[:, :COLS] + noise_var * rhs
    shared = lanes(jnp.pad(images, ((0, 0), (0, 1))), summed[:, 32:96])
    col_got = gather_blocks(shared, "row")
    row_got = gather_blocks(jnp.pad(images, ((0, 0), (0, 1))), "col")
    col_v = col_got[:, :, :COLS].reshape(row_count * width, COLS)
    row_v = row_got[:, :, :COLS].reshape(col_count * width, COLS)
    grams = jnp.sum(col_got[:, :, 32:96], 0)
    res_gram = symmetric(grams[:COLS, 32 : 32 + COLS])
    curvature = symmetric(signal_var * grams[:COLS, :COLS] + noise_var * res_gram)
    advance = solve_spd(curvature, res_gram)

    def residual_of(rhs_part, image_part):
        return rhs_part - mul("nc,cd->nd", image_part, advance)

    row_r, col_r, own_r = residual_of(row_b, row_v), residual_of(col_b, col_v), residual_of(rhs, images)
    product = mul("mn,nc->mc", base, col_r)
    message = lanes(
        square32(mul("mc,md->cd", row_r, product)),
        square32(mul("mc,md->cd", own_r, own_r)),
        square32(mul("mc,md->cd", images, own_r)),
    )
    sums = sum_blocks(sum_blocks(message, "col"), "row")
    next_gram = symmetric(sums[:COLS, 32 : 32 + COLS])
    cross = sums[:COLS, 64 : 64 + COLS]
    carry_over = solve_spd(res_gram, next_gram)
    mixed = mul("cd,ce->de", cross, carry_over)
    next_curv = symmetric(
        signal_var * sums[:COLS, :COLS]
        + noise_var * next_gram
        + mixed
        + mixed.T
        + mul("cd,ce->de", carry_over, mul("cd,de->ce", curvature, carry_over))
    )
    next_advance = solve_spd(next_curv, next_gram)
    rhs_coef = advance + mul("cd,de->ce", carry_over, next_advance)

    def solves_of(rhs_part, res_part, cut=slice(None)):
        return mul("nc,cd->nd", rhs_part, rhs_coef[:, cut]) + mul("nc,cd->nd", res_part, next_advance[:, cut])

    own_s, row_s = solves_of(rhs, own_r), solves_of(row_b, row_r)
    col_s = solves_of(col_b, col_r, slice(PROBES, COLS))
    weights = jnp.where(jnp.arange(COLS) < PROBES, -1.0 / PROBES, 1.0) * (0.5 / total_points)
    row_w = row_s * weights[None, :]
    col_pair = jnp.concatenate([col_b[:, :PROBES], col_s], 1)
    matrix = mul("mc,nc->mn", row_w, col_pair)
    weighted = matrix * slope
    right = jnp.concatenate([col_x, col_x * col_x, jnp.ones((col_x.shape[0], 1), jnp.float32)], 1)
    moved = mul("mn,nf->mf", weighted, right)
    scale_terms = jnp.sum(
        row_x * row_x * moved[:, 2 * FEAT :] + moved[:, FEAT : 2 * FEAT] - 2.0 * row_x * moved[:, :FEAT], 0
    )
    signal_term = jnp.sum(matrix * base)
    noise_term = noise_var * jnp.sum(own_s * weights[None, :] * jnp.concatenate([rhs[:, :PROBES], own_s[:, PROBES:]], 1))
    terms = jnp.concatenate(
        [signal_var * scale_terms, (signal_var * signal_term)[None], noise_term[None], jnp.zeros((62,), jnp.float32)]
    )
    gradient = sum_blocks(sum_blocks(terms[None], "col"), "row")[0, : FEAT + 2]
    return (own_s.T, gradient)


def solution(mesh):
    placed = (P(None, ("row", "col")), P(), P(), P(("row", "col")), P(None, ("row", "col")))
    return jax.shard_map(
        local, mesh=mesh, in_specs=placed, out_specs=(P(None, ("row", "col")), P()), check_vma=False
    )
```

```python
import functools

import jax
import jax.numpy as jnp
from jax import lax
from jax.experimental import pallas as pl
from jax.experimental.pallas import tpu as pltpu
from jax.sharding import PartitionSpec as P

PROBES = 30
COLS = 31
FEAT = 64
PAD = 32
f32 = jnp.float32
highest = lax.Precision.HIGHEST
PARAMS = pltpu.CompilerParams(vmem_limit_bytes=48 * 1024 * 1024)


def dot(left, right, left_dim=1, right_dim=0):
    return lax.dot_general(
        left, right, (((left_dim,), (right_dim,)), ((), ())), precision=highest, preferred_element_type=f32
    )


def pack(square):
    return jnp.concatenate([square[8 * g : 8 * g + 8] for g in range(4)], 1)


def unpack(rows):
    return jnp.concatenate([rows[:, PAD * g : PAD * g + PAD] for g in range(4)], 0)


def unpack_columns(ref, start):
    count = ref.shape[0]
    pieces = [ref[:, start : start + 8, PAD * g : PAD * g + PAD].reshape(8 * count, PAD) for g in range(4)]
    return jnp.concatenate(pieces, 0)


def unpack_points(ref):
    count = ref.shape[0]
    pieces = []
    for g in range(4):
        top, left = 8 * (g // 2), FEAT * (g % 2)
        pieces.append(ref[:, top : top + 8, left : left + FEAT].reshape(8 * count, FEAT))
    return jnp.concatenate(pieces, 0)


def places(rows=PAD, columns=PAD):
    shape = (rows, columns)
    return lax.broadcasted_iota(jnp.int32, shape, 0), lax.broadcasted_iota(jnp.int32, shape, 1)


def symmetric(matrix):
    return 0.5 * (matrix + matrix.T)


def join_symmetric(first, second):
    down, across = places()
    diagonal = jnp.sum(jnp.where(down == across, second, 0.0), 0, keepdims=True)
    return jnp.where(down == PAD - 1, diagonal, jnp.where(down >= across, first, second))


def part_symmetric(joined):
    down, across = places()
    inside = down < PAD - 1
    lower = jnp.where((down >= across) & inside, joined, 0.0)
    upper = jnp.where(down < across, joined, 0.0)
    eye = down == across
    first = jnp.where(eye, lower, lower + lower.T)
    second = upper + upper.T + jnp.where(eye, joined[PAD - 1 : PAD, :], 0.0)
    return first, second


def eliminate(systems):
    down = lax.broadcasted_iota(jnp.int32, (PAD, 1), 0)
    for k in range(COLS):
        for n, system in enumerate(systems):
            row = system[k : k + 1, :] * (1.0 / system[k : k + 1, k : k + 1])
            column = jnp.where(down == k, 0.0, system[:, k : k + 1])
            kept = jnp.where(down == k, row, system)
            systems[n] = kept - column * row
    return [system[:, PAD:] for system in systems]


def identity():
    down, across = places()
    return jnp.where(down == across, 1.0, 0.0)


def start_kernel(points_ref, lengths_ref, probes_ref, targets_ref, row_ref, col_ref):
    scaled = points_ref[...] / lengths_ref[...]
    rhs = jnp.concatenate([probes_ref[...], targets_ref[...], jnp.zeros((1, PAD), f32)], 0).T
    pairs = [jnp.concatenate([scaled[16 * g : 16 * g + 8], scaled[16 * g + 8 : 16 * g + 16]], 1) for g in range(2)]
    block = jnp.concatenate(pairs + [pack(rhs)], 0)
    row_ref[...] = jnp.broadcast_to(block[None], row_ref.shape)
    col_ref[...] = jnp.broadcast_to(block[None], col_ref.shape)


def augmented(points, last, one):
    norm = jnp.sum(points * points, 1, keepdims=True)
    across = lax.broadcasted_iota(jnp.int32, (points.shape[0], FEAT), 1)
    tail = jnp.where(across == last, norm, jnp.where(across == one, 1.0, 0.0))
    return jnp.concatenate([points, tail], 1)


def tile_kernel(row_ref, col_ref, own_ref, base_ref, slope_ref, message_ref):
    row_points = unpack_points(row_ref)
    col_points = unpack_points(col_ref)
    left = augmented(row_points, 0, 1)
    right = augmented(col_points, 1, 0)
    across = lax.broadcasted_iota(jnp.int32, right.shape, 1)
    right = jnp.where(across < FEAT, -10.0 * right, 5.0 * right)
    base_ref[...] = dot(left, right, 1, 1)

    def strip(i, carry):
        here = pl.ds(pl.multiple_of(i * 16, 16), 16)
        squared = jnp.maximum(base_ref[here, :], 0.0)
        dist = squared * lax.rsqrt(jnp.maximum(squared, 1e-30))
        decayed = jnp.exp(-dist)
        more = 1.0 + dist
        slope_ref[here, :] = more * decayed
        base_ref[here, :] = (more + squared * (1.0 / 3.0)) * decayed
        return carry

    lax.fori_loop(0, base_ref.shape[0] // 16, strip, 0)
    row_rhs = unpack_columns(row_ref, 16)
    col_rhs = unpack_columns(col_ref, 16)
    own_rhs = unpack(own_ref[16:24, :])
    partial = dot(base_ref[...], col_rhs)
    curvature = dot(row_rhs, partial, 0, 0)
    gram = dot(own_rhs, own_rhs, 0, 0)
    quarter = partial.shape[0] // 4
    chunks = jnp.concatenate([partial[quarter * g : quarter * g + quarter] for g in range(4)], 1)
    message_ref[:, 0:8, :] = chunks.reshape(quarter // 8, 8, 128)
    grams = pack(join_symmetric(symmetric(curvature), gram))
    message_ref[:, 8:16, :] = jnp.broadcast_to(grams[None], (quarter // 8, 8, 128))


def images_kernel(variances_ref, got_ref, own_ref, row_ref, col_ref):
    summed = jnp.sum(got_ref[...], 0)
    images = variances_ref[0] * summed[0:8] + variances_ref[1] * own_ref[16:24, :]
    row_ref[...] = jnp.broadcast_to(images[None], row_ref.shape)
    col_ref[...] = jnp.broadcast_to(jnp.concatenate([images, summed[8:16]], 0)[None], col_ref.shape)


def advance_kernel(variances_ref, got_ref, col_ref, base_ref, advance_ref, inverse_ref, curvature_ref, res_ref, product_ref):
    base_curvature, res_gram = part_symmetric(unpack(jnp.sum(got_ref[:, 8:16, :], 0)))
    curvature = variances_ref[0] * base_curvature + variances_ref[1] * res_gram
    advance, inverse = eliminate(
        [jnp.concatenate([curvature, res_gram], 1), jnp.concatenate([res_gram, identity()], 1)]
    )
    residual = unpack_columns(col_ref, 16) - dot(unpack_columns(got_ref, 0), advance)
    res_ref[...] = residual
    advance_ref[...] = advance
    inverse_ref[...] = inverse
    curvature_ref[...] = curvature
    product_ref[...] = dot(base_ref[...], residual)


def grams_kernel(got_ref, row_ref, own_ref, images_ref, advance_ref, product_ref, res_ref, own_res_ref, message_ref):
    advance = advance_ref[...]
    residual = unpack_columns(row_ref, 16) - dot(unpack_columns(got_ref, 0), advance)
    res_ref[...] = residual
    own_res = unpack(own_ref[16:24, :]) - dot(unpack(images_ref[0]), advance)
    own_res_ref[...] = own_res
    curvature = dot(residual, product_ref[...], 0, 0)
    gram = dot(own_res, own_res, 0, 0)
    message = pack(join_symmetric(symmetric(curvature), gram))
    message_ref[...] = jnp.broadcast_to(message[None], message_ref.shape)


def gradient_kernel(
    total_points,
    variances_ref,
    got_ref,
    advance_ref,
    inverse_ref,
    curvature_ref,
    row_ref,
    col_ref,
    own_ref,
    row_res_ref,
    col_res_ref,
    own_res_ref,
    base_ref,
    slope_ref,
    solves_ref,
    terms_ref,
    matrix_ref,
):
    signal_var, noise_var = variances_ref[0], variances_ref[1]
    base_curvature, next_gram = part_symmetric(unpack(jnp.sum(got_ref[...], 0)))
    carry_over = dot(inverse_ref[...], next_gram)
    next_curv = (
        signal_var * base_curvature
        + noise_var * next_gram
        - symmetric(dot(carry_over, dot(curvature_ref[...], carry_over), 0, 0))
    )
    (next_advance,) = eliminate([jnp.concatenate([next_curv, next_gram], 1)])
    rhs_coef = advance_ref[...] + dot(carry_over, next_advance)

    def solves_of(rhs, residual):
        return dot(rhs, rhs_coef) + dot(residual, next_advance)

    def pair_of(rhs, solves):
        across = lax.broadcasted_iota(jnp.int32, rhs.shape, 1)
        return jnp.where(across < PROBES, rhs, solves)

    own_rhs = unpack(own_ref[16:24, :])
    own_solves = solves_of(own_rhs, own_res_ref[...])
    solves_ref[...] = own_solves.T[0:COLS, :]
    col_rhs = unpack_columns(col_ref, 16)
    col_pair = pair_of(col_rhs, solves_of(col_rhs, col_res_ref[...]))
    across = lax.broadcasted_iota(jnp.int32, (1, PAD), 1)
    weights = jnp.where(across < PROBES, -1.0 / PROBES, 1.0) * (0.5 / total_points)
    row_weights = solves_of(unpack_columns(row_ref, 16), row_res_ref[...]) * weights
    matrix_ref[...] = dot(row_weights, col_pair, 1, 1)

    def strip(i, total):
        here = pl.ds(pl.multiple_of(i * 16, 16), 16)
        values = matrix_ref[here, :]
        matrix_ref[here, :] = values * slope_ref[here, :]
        return total + values * base_ref[here, :]

    signal = lax.fori_loop(0, matrix_ref.shape[0] // 16, strip, jnp.zeros((16, matrix_ref.shape[1]), f32))
    row_points = unpack_points(row_ref)
    col_points = unpack_points(col_ref)
    right = jnp.concatenate([col_points, col_points * col_points, jnp.ones((col_points.shape[0], 128), f32)], 1)
    moved = dot(matrix_ref[...], right)
    scales = row_points * (row_points * moved[:, 128 : 128 + FEAT] - 2.0 * moved[:, :FEAT]) + moved[:, FEAT:128]
    scale_terms = (5.0 / 3.0 * signal_var) * jnp.sum(scales, 0, keepdims=True)
    signal_term = signal_var * jnp.sum(jnp.sum(signal, 0, keepdims=True), 1, keepdims=True)
    noise = jnp.sum(own_solves * weights * pair_of(own_rhs, own_solves), 0, keepdims=True)
    noise_term = noise_var * jnp.sum(noise, 1, keepdims=True)
    terms_ref[...] = jnp.concatenate([scale_terms, signal_term, noise_term, jnp.zeros((1, FEAT - 2), f32)], 1)


def shape_of(*dims):
    return jax.ShapeDtypeStruct(dims, f32)


def call(kernel, outs, *operands, scalars=0, scratch=(), flops=1):
    smem = [pl.BlockSpec(memory_space=pltpu.SMEM)] * scalars
    vmem = [pl.BlockSpec(memory_space=pltpu.VMEM)] * (len(operands) - scalars)
    return pl.pallas_call(
        kernel,
        out_shape=outs,
        in_specs=smem + vmem,
        out_specs=[pl.BlockSpec(memory_space=pltpu.VMEM)] * len(outs),
        scratch_shapes=scratch,
        compiler_params=PARAMS,
        cost_estimate=pl.CostEstimate(flops=flops, bytes_accessed=1 << 20, transcendentals=0),
    )(*operands)


def exchange(blocks, axis):
    return lax.all_to_all(blocks, axis, 0, 0, tiled=True)


def local(points, length_scales, variances, targets, probe_vectors):
    rows = lax.axis_size("row")
    cols = lax.axis_size("col")
    width = points.shape[1]
    row_block, col_set = cols * width, rows * width
    total_points = width * rows * cols
    to_row, to_col = call(
        start_kernel,
        [shape_of(cols, 24, 128), shape_of(rows, 24, 128)],
        points.T,
        length_scales[None],
        probe_vectors,
        targets[None],
    )
    own = to_row[0]
    row_got = exchange(to_row, "col")
    col_got = exchange(to_col, "row")
    base, slope, message = call(
        tile_kernel,
        [shape_of(row_block, col_set), shape_of(row_block, col_set), shape_of(cols, 16, 128)],
        row_got,
        col_got,
        own,
    )
    images_row, images_col = call(
        images_kernel,
        [shape_of(cols, 8, 128), shape_of(rows, 16, 128)],
        variances,
        exchange(message, "col"),
        own,
        scalars=1,
    )
    images_col_got = exchange(images_col, "row")
    images_row_got = exchange(images_row, "col")
    square = shape_of(PAD, PAD)
    advance, inverse, curvature, col_res, product = call(
        advance_kernel,
        [square, square, square, shape_of(col_set, PAD), shape_of(row_block, PAD)],
        variances,
        images_col_got,
        col_got,
        base,
        scalars=1,
    )
    row_res, own_res, message = call(
        grams_kernel,
        [shape_of(row_block, PAD), square, shape_of(cols, 8, 128)],
        images_row_got,
        row_got,
        own,
        images_row,
        advance,
        product,
    )
    summed = jnp.sum(exchange(message, "col"), 0)
    grams_got = exchange(jnp.broadcast_to(summed[None], (rows, 8, 128)), "row")
    solves, terms = call(
        functools.partial(gradient_kernel, total_points),
        [shape_of(COLS, width), shape_of(1, 128)],
        variances,
        grams_got,
        advance,
        inverse,
        curvature,
        row_got,
        col_got,
        own,
        row_res,
        col_res,
        own_res,
        base,
        slope,
        scalars=1,
        scratch=[pltpu.VMEM((row_block, col_set), f32)],
    )
    terms = jnp.sum(exchange(jnp.broadcast_to(terms[None], (cols, 1, 128)), "col"), 0)
    terms = jnp.sum(exchange(jnp.broadcast_to(terms[None], (rows, 1, 128)), "row"), 0)
    return (solves, terms[0, : FEAT + 2])


def solution(mesh):
    placed = (P(None, ("row", "col")), P(), P(), P(("row", "col")), P(None, ("row", "col")))
    return jax.shard_map(
        local, mesh=mesh, in_specs=placed, out_specs=(P(None, ("row", "col")), P()), check_vma=False
    )
```

```python
import functools

import jax
import jax.numpy as jnp
from jax import lax
from jax.experimental import pallas as pl
from jax.experimental.pallas import tpu as pltpu
from jax.sharding import PartitionSpec as P

PROBES = 30
COLS = 31
FEAT = 64
PAD = 32
f32 = jnp.float32
bf16 = jnp.bfloat16
root_five = 5.0**0.5
highest = lax.Precision.HIGHEST
PARAMS = pltpu.CompilerParams(vmem_limit_bytes=32 * 1024 * 1024)


def dot(left, right, left_dim=1, right_dim=0):
    return lax.dot_general(
        left, right, (((left_dim,), (right_dim,)), ((), ())), precision=highest, preferred_element_type=f32
    )


def pack(square):
    return jnp.concatenate([square[8 * g : 8 * g + 8] for g in range(4)], 1)


def unpack(rows):
    return jnp.concatenate([rows[:, PAD * g : PAD * g + PAD] for g in range(4)], 0)


def unpack_columns(ref, start):
    count = ref.shape[0]
    pieces = [ref[:, start : start + 8, PAD * g : PAD * g + PAD].reshape(8 * count, PAD) for g in range(4)]
    return jnp.concatenate(pieces, 0)


def unpack_points(ref):
    count = ref.shape[0]
    pieces = []
    for g in range(4):
        top, left = 8 * (g // 2), FEAT * (g % 2)
        pieces.append(ref[:, top : top + 8, left : left + FEAT].reshape(8 * count, FEAT))
    return jnp.concatenate(pieces, 0)


def places(rows=PAD, columns=PAD):
    shape = (rows, columns)
    return lax.broadcasted_iota(jnp.int32, shape, 0), lax.broadcasted_iota(jnp.int32, shape, 1)


def symmetric(matrix):
    return 0.5 * (matrix + matrix.T)


def join_symmetric(first, second):
    down, across = places()
    diagonal = jnp.sum(jnp.where(down == across, second, 0.0), 0, keepdims=True)
    return jnp.where(down == PAD - 1, diagonal, jnp.where(down >= across, first, second))


def part_symmetric(joined):
    down, across = places()
    inside = down < PAD - 1
    lower = jnp.where((down >= across) & inside, joined, 0.0)
    upper = jnp.where(down < across, joined, 0.0)
    eye = down == across
    first = jnp.where(eye, lower, lower + lower.T)
    second = upper + upper.T + jnp.where(eye, joined[PAD - 1 : PAD, :], 0.0)
    return first, second


def eliminate(systems):
    down = lax.broadcasted_iota(jnp.int32, (PAD, 1), 0)
    for k in range(COLS):
        for n, system in enumerate(systems):
            row = system[k : k + 1, :] * (1.0 / system[k : k + 1, k : k + 1])
            column = jnp.where(down == k, 0.0, system[:, k : k + 1])
            kept = jnp.where(down == k, row, system)
            systems[n] = kept - column * row
    return [system[:, PAD:] for system in systems]


def identity():
    down, across = places()
    return jnp.where(down == across, 1.0, 0.0)


def pieces_of(array, count=3):
    pieces = []
    for _ in range(count):
        piece = array.astype(bf16)
        pieces.append(piece)
        array = array - piece.astype(f32)
    return pieces


def bdot(left, right, right_dim=0):
    return lax.dot_general(left, right, (((1,), (right_dim,)), ((), ())), preferred_element_type=f32)


def left_pieces(array):
    high, mid, low = pieces_of(array)
    return jnp.concatenate([high, high, high, mid, mid, low], 1)


def right_pieces(array, dim):
    high, mid, low = pieces_of(array)
    return jnp.concatenate([high, mid, low, high, mid, high], dim)


def wide_dot(left, right, right_dim=0):
    return bdot(left_pieces(left), right_pieces(right, right_dim), right_dim)


def tile_dot(high_ref, mid_ref, low_ref, right):
    first, second, third = pieces_of(right)
    both = jnp.concatenate([first, second], 1)
    by_high = bdot(high_ref[...], jnp.concatenate([both, third], 1))
    by_mid = bdot(mid_ref[...], both)
    by_low = bdot(low_ref[...], first)
    small = by_high[:, 2 * PAD :] + by_mid[:, PAD:] + by_low
    return by_high[:, :PAD] + (by_high[:, PAD : 2 * PAD] + by_mid[:, :PAD] + small)


def start_copies(sources, targets, sems):
    copies = [pltpu.make_async_copy(s, t, sems.at[n]) for n, (s, t) in enumerate(zip(sources, targets))]
    for copy in copies:
        copy.start()
    return copies


def start_kernel(
    points_hbm, lengths_hbm, probes_hbm, targets_hbm, own_ref, col_ref, points_ref, lengths_ref, probes_ref, targets_ref, sems
):
    refs = (points_ref, lengths_ref, probes_ref, targets_ref)
    for copy in start_copies((points_hbm, lengths_hbm, probes_hbm, targets_hbm), refs, sems):
        copy.wait()
    scaled = points_ref[...] / lengths_ref[...]
    rhs = jnp.concatenate([probes_ref[...], targets_ref[...], jnp.zeros((1, PAD), f32)], 0).T
    pairs = [jnp.concatenate([scaled[16 * g : 16 * g + 8], scaled[16 * g + 8 : 16 * g + 16]], 1) for g in range(2)]
    block = jnp.concatenate(pairs + [pack(rhs)], 0)
    own_ref[...] = block
    col_ref[...] = jnp.broadcast_to(block[None], col_ref.shape)


def norm_lanes(points, first):
    across = lax.broadcasted_iota(jnp.int32, (points.shape[0], 128), 1)
    lanes = jnp.where((across >= 3 - first) & (across < 6 - first), 1.0, 0.0)
    for n, piece in enumerate(pieces_of(jnp.sum(points * points, 1, keepdims=True))):
        lanes = jnp.where(across == first + n, piece.astype(f32), lanes)
    return lanes.astype(bf16)


def tile_kernel(
    row_ref, col_ref, own_ref, slope_hbm, high_hbm, mid_hbm, low_hbm, message_ref, slope_ref, high_ref, mid_ref, low_ref, sems
):
    row_points = unpack_points(row_ref) * root_five
    col_points = unpack_points(col_ref) * root_five
    left = jnp.concatenate([left_pieces(row_points), norm_lanes(row_points, 0)], 1)
    right = jnp.concatenate([right_pieces(-2.0 * col_points, 1), norm_lanes(col_points, 3)], 1)
    slope_ref[...] = bdot(left, right, 1)

    def strip(i, carry):
        here = pl.ds(pl.multiple_of(i * 16, 16), 16)
        squared = jnp.maximum(slope_ref[here, :], 0.0)
        dist = squared * lax.rsqrt(jnp.maximum(squared, 1e-30))
        decayed = jnp.exp(-dist)
        more = 1.0 + dist
        slope_ref[here, :] = more * decayed
        high, mid, low = pieces_of((more + squared * (1.0 / 3.0)) * decayed)
        high_ref[here, :] = high
        mid_ref[here, :] = mid
        low_ref[here, :] = low
        return carry

    lax.fori_loop(0, slope_ref.shape[0] // 16, strip, 0)
    copies = start_copies((slope_ref, high_ref, mid_ref, low_ref), (slope_hbm, high_hbm, mid_hbm, low_hbm), sems)
    row_rhs = unpack_columns(row_ref, 16)
    col_rhs = unpack_columns(col_ref, 16)
    own_rhs = unpack(own_ref[16:24, :])
    partial = tile_dot(high_ref, mid_ref, low_ref, col_rhs)
    curvature = dot(row_rhs, partial, 0, 0)
    gram = dot(own_rhs, own_rhs, 0, 0)
    quarter = partial.shape[0] // 4
    chunks = jnp.concatenate([partial[quarter * g : quarter * g + quarter] for g in range(4)], 1)
    message_ref[:, 0:8, :] = chunks.reshape(quarter // 8, 8, 128)
    grams = pack(join_symmetric(symmetric(curvature), gram))
    message_ref[:, 8:16, :] = jnp.broadcast_to(grams[None], (quarter // 8, 8, 128))
    for copy in copies:
        copy.wait()


def images_kernel(variances_ref, got_ref, own_ref, own_images_ref, row_ref, col_ref):
    summed = jnp.sum(got_ref[...], 0)
    images = variances_ref[0] * summed[0:8] + variances_ref[1] * own_ref[16:24, :]
    own_images_ref[...] = images
    row_ref[...] = jnp.broadcast_to(images[None], row_ref.shape)
    col_ref[...] = jnp.broadcast_to(jnp.concatenate([images, summed[8:16]], 0)[None], col_ref.shape)


def residual_of(rhs, images, advance):
    return rhs - wide_dot(images, advance)


def advance_kernel(
    variances_ref, got_ref, col_ref, high_hbm, mid_hbm, low_hbm, coef_ref, product_ref, high_ref, mid_ref, low_ref, sems
):
    copies = start_copies((high_hbm, mid_hbm, low_hbm), (high_ref, mid_ref, low_ref), sems)
    base_curvature, res_gram = part_symmetric(unpack(jnp.sum(got_ref[:, 8:16, :], 0)))
    curvature = variances_ref[0] * base_curvature + variances_ref[1] * res_gram
    advance, inverse = eliminate(
        [jnp.concatenate([curvature, res_gram], 1), jnp.concatenate([res_gram, identity()], 1)]
    )
    coef_ref[...] = jnp.concatenate([advance, inverse, curvature, jnp.zeros((PAD, PAD), f32)], 1)
    residual = residual_of(unpack_columns(col_ref, 16), unpack_columns(got_ref, 0), advance)
    for copy in copies:
        copy.wait()
    product_ref[...] = tile_dot(high_ref, mid_ref, low_ref, residual)


def grams_kernel(got_ref, row_ref, own_ref, own_images_ref, coef_ref, product_ref, message_ref):
    advance = coef_ref[:, :PAD]
    residual = residual_of(unpack_columns(row_ref, 16), unpack_columns(got_ref, 0), advance)
    own_res = residual_of(unpack(own_ref[16:24, :]), unpack(own_images_ref[...]), advance)
    curvature = dot(residual, product_ref[...], 0, 0)
    gram = dot(own_res, own_res, 0, 0)
    message = pack(join_symmetric(symmetric(curvature), gram))
    message_ref[...] = jnp.broadcast_to(message[None], message_ref.shape)


def spread_kernel(got_ref, out_ref):
    out_ref[...] = jnp.broadcast_to(jnp.sum(got_ref[...], 0)[None], out_ref.shape)


def gradient_kernel(
    total_points,
    variances_ref,
    got_ref,
    coef_ref,
    row_ref,
    col_ref,
    own_ref,
    row_images_ref,
    col_images_ref,
    own_images_ref,
    slope_hbm,
    high_hbm,
    mid_hbm,
    solves_ref,
    terms_ref,
    slope_ref,
    high_ref,
    mid_ref,
    matrix_ref,
    upper_ref,
    lower_ref,
    sums_ref,
    sems,
):
    copies = start_copies((slope_hbm, high_hbm, mid_hbm), (slope_ref, high_ref, mid_ref), sems)
    signal_var, noise_var = variances_ref[0], variances_ref[1]
    advance, inverse, curvature = (coef_ref[:, PAD * g : PAD * g + PAD] for g in range(3))
    base_curvature, next_gram = part_symmetric(unpack(jnp.sum(got_ref[...], 0)))
    carry_over = dot(inverse, next_gram)
    next_curv = (
        signal_var * base_curvature
        + noise_var * next_gram
        - symmetric(dot(carry_over, dot(curvature, carry_over), 0, 0))
    )
    (next_advance,) = eliminate([jnp.concatenate([next_curv, next_gram], 1)])
    rhs_coef = advance + dot(carry_over + identity(), next_advance)
    coef = jnp.concatenate([rhs_coef, -dot(advance, next_advance)], 0)

    def solves_of(rhs, images):
        return wide_dot(jnp.concatenate([rhs, images], 1), coef)

    def pair_of(rhs, solves):
        across = lax.broadcasted_iota(jnp.int32, rhs.shape, 1)
        return jnp.where(across < PROBES, rhs, solves)

    own_rhs = unpack(own_ref[16:24, :])
    own_solves = solves_of(own_rhs, unpack(own_images_ref[...]))
    solves_ref[...] = own_solves.T[0:COLS, :]
    col_rhs = unpack_columns(col_ref, 16)
    col_pair = pair_of(col_rhs, solves_of(col_rhs, unpack_columns(col_images_ref, 0)))
    across = lax.broadcasted_iota(jnp.int32, (1, PAD), 1)
    weights = jnp.where(across < PROBES, -1.0 / PROBES, 1.0) * (0.5 / total_points)
    row_weights = solves_of(unpack_columns(row_ref, 16), unpack_columns(row_images_ref, 0)) * weights
    matrix_ref[...] = wide_dot(row_weights, col_pair, 1)
    for copy in copies:
        copy.wait()

    def strip(i, total):
        here = pl.ds(pl.multiple_of(i * 16, 16), 16)
        values = matrix_ref[here, :]
        weighted = values * slope_ref[here, :]
        upper = weighted.astype(bf16)
        upper_ref[here, :] = upper
        lower_ref[here, :] = (weighted - upper.astype(f32)).astype(bf16)
        sums_ref[here, :] = jnp.broadcast_to(jnp.sum(weighted, 1, keepdims=True), (16, 128))
        return total + values * (high_ref[here, :].astype(f32) + mid_ref[here, :].astype(f32))

    signal = lax.fori_loop(0, matrix_ref.shape[0] // 16, strip, jnp.zeros((16, matrix_ref.shape[1]), f32))
    row_points = unpack_points(row_ref)
    col_points = unpack_points(col_ref)
    right_high, right_low = pieces_of(jnp.concatenate([col_points, col_points * col_points], 1), 2)
    by_upper = bdot(upper_ref[...], jnp.concatenate([right_high, right_low], 1))
    moved = by_upper[:, :128] + (by_upper[:, 128:] + bdot(lower_ref[...], right_high))
    scales = row_points * (row_points * sums_ref[:, :FEAT] - 2.0 * moved[:, :FEAT]) + moved[:, FEAT:128]
    scale_terms = (5.0 / 3.0 * signal_var) * jnp.sum(scales, 0, keepdims=True)
    signal_term = signal_var * jnp.sum(jnp.sum(signal, 0, keepdims=True), 1, keepdims=True)
    noise = jnp.sum(own_solves * weights * pair_of(own_rhs, own_solves), 0, keepdims=True)
    noise_term = noise_var * jnp.sum(noise, 1, keepdims=True)
    terms_ref[...] = jnp.concatenate([scale_terms, signal_term, noise_term, jnp.zeros((1, FEAT - 2), f32)], 1)


def shape_of(*dims, dtype=f32):
    return jax.ShapeDtypeStruct(dims, dtype)


def call(kernel, outs, *operands, scalars=0, far_in=0, far_outs=0, scratch=(), flops=1):
    scalar, near, far = (pl.BlockSpec(memory_space=m) for m in (pltpu.SMEM, pltpu.VMEM, pltpu.HBM))
    near_in = len(operands) - scalars - far_in
    return pl.pallas_call(
        kernel,
        out_shape=outs,
        in_specs=[scalar] * scalars + [near] * near_in + [far] * far_in,
        out_specs=[far] * far_outs + [near] * (len(outs) - far_outs),
        scratch_shapes=scratch,
        compiler_params=PARAMS,
        cost_estimate=pl.CostEstimate(flops=flops, bytes_accessed=1 << 20, transcendentals=0),
    )(*operands)


def exchange(blocks, axis):
    return lax.all_to_all(blocks, axis, 0, 0, tiled=True)


def local(points, length_scales, variances, targets, probe_vectors):
    rows = lax.axis_size("row")
    cols = lax.axis_size("col")
    width = points.shape[1]
    row_block, col_set = cols * width, rows * width
    total_points = width * rows * cols
    tile = (row_block, col_set)
    sems = pltpu.SemaphoreType.DMA((4,))
    values, halves = pltpu.VMEM(tile, f32), pltpu.VMEM(tile, bf16)
    own, to_col = call(
        start_kernel,
        [shape_of(24, 128), shape_of(rows, 24, 128)],
        points.T,
        length_scales[None],
        probe_vectors,
        targets[None],
        far_in=4,
        scratch=[
            pltpu.VMEM((width, FEAT), f32),
            pltpu.VMEM((1, FEAT), f32),
            pltpu.VMEM((PROBES, width), f32),
            pltpu.VMEM((1, width), f32),
            sems,
        ],
    )
    col_got = exchange(to_col, "row")
    row_got = lax.all_gather(own, "col")
    slope, high, mid, low, message = call(
        tile_kernel,
        [shape_of(*tile)] + [shape_of(*tile, dtype=bf16)] * 3 + [shape_of(cols, 16, 128)],
        row_got,
        col_got,
        own,
        far_outs=4,
        scratch=[values, halves, halves, halves, sems],
    )
    own_images, images_row, images_col = call(
        images_kernel,
        [shape_of(8, 128), shape_of(cols, 8, 128), shape_of(rows, 16, 128)],
        variances,
        exchange(message, "col"),
        own,
        scalars=1,
    )
    col_images = exchange(images_col, "row")
    row_images = exchange(images_row, "col")
    coef, product = call(
        advance_kernel,
        [shape_of(PAD, 128), shape_of(row_block, PAD)],
        variances,
        col_images,
        col_got,
        high,
        mid,
        low,
        scalars=1,
        far_in=3,
        scratch=[halves, halves, halves, sems],
    )
    (message,) = call(
        grams_kernel, [shape_of(cols, 8, 128)], row_images, row_got, own, own_images, coef, product
    )
    (message,) = call(spread_kernel, [shape_of(rows, 8, 128)], exchange(message, "col"))
    solves, terms = call(
        functools.partial(gradient_kernel, total_points),
        [shape_of(COLS, width), shape_of(1, 128)],
        variances,
        exchange(message, "row"),
        coef,
        row_got,
        col_got,
        own,
        row_images,
        col_images,
        own_images,
        slope,
        high,
        mid,
        scalars=1,
        far_in=3,
        scratch=[values, halves, halves, values, halves, halves, pltpu.VMEM((row_block, 128), f32), sems],
    )
    terms = jnp.sum(exchange(jnp.broadcast_to(terms[None], (cols, 1, 128)), "col"), 0)
    terms = jnp.sum(exchange(jnp.broadcast_to(terms[None], (rows, 1, 128)), "row"), 0)
    return (solves, terms[0, : FEAT + 2])


def solution(mesh):
    placed = (P(None, ("row", "col")), P(), P(), P(("row", "col")), P(None, ("row", "col")))
    return jax.shard_map(
        local, mesh=mesh, in_specs=placed, out_specs=(P(None, ("row", "col")), P()), check_vma=False
    )
```

```python
import functools

import jax
import jax.numpy as jnp
from jax import lax
from jax.experimental import pallas as pl
from jax.experimental.pallas import tpu as pltpu
from jax.sharding import PartitionSpec as P

PROBES = 30
COLS = 31
FEAT = 64
PAD = 32
PARTS = 4
f32 = jnp.float32
bf16 = jnp.bfloat16
root_five = 5.0**0.5
highest = lax.Precision.HIGHEST
PARAMS = pltpu.CompilerParams(vmem_limit_bytes=60 * 1024 * 1024)


def dot(left, right, left_dim=1, right_dim=0):
    return lax.dot_general(
        left, right, (((left_dim,), (right_dim,)), ((), ())), precision=highest, preferred_element_type=f32
    )


def pack(square):
    return jnp.concatenate([square[8 * g : 8 * g + 8] for g in range(4)], 1)


def unpack(rows):
    return jnp.concatenate([rows[:, PAD * g : PAD * g + PAD] for g in range(4)], 0)


def unpack_columns(ref, start):
    count = ref.shape[0]
    pieces = [ref[:, start : start + 8, PAD * g : PAD * g + PAD].reshape(8 * count, PAD) for g in range(4)]
    return jnp.concatenate(pieces, 0)


def unpack_points(ref):
    count = ref.shape[0]
    pieces = []
    for g in range(4):
        top, left = 8 * (g // 2), FEAT * (g % 2)
        pieces.append(ref[:, top : top + 8, left : left + FEAT].reshape(8 * count, FEAT))
    return jnp.concatenate(pieces, 0)


def places(rows=PAD, columns=PAD):
    shape = (rows, columns)
    return lax.broadcasted_iota(jnp.int32, shape, 0), lax.broadcasted_iota(jnp.int32, shape, 1)


def symmetric(matrix):
    return 0.5 * (matrix + matrix.T)


def join_symmetric(first, second):
    down, across = places()
    diagonal = jnp.sum(jnp.where(down == across, second, 0.0), 0, keepdims=True)
    return jnp.where(down == PAD - 1, diagonal, jnp.where(down >= across, first, second))


def part_symmetric(joined):
    down, across = places()
    inside = down < PAD - 1
    lower = jnp.where((down >= across) & inside, joined, 0.0)
    upper = jnp.where(down < across, joined, 0.0)
    eye = down == across
    first = jnp.where(eye, lower, lower + lower.T)
    second = upper + upper.T + jnp.where(eye, joined[PAD - 1 : PAD, :], 0.0)
    return first, second


def eliminate(systems):
    down, across = places(PAD, 2 * PAD)
    systems = [jnp.where((down == PAD - 1) & (across == PAD - 1), 1.0, system) for system in systems]
    for k in range(0, PAD, 2):
        first, second = down == k, down == k + 1
        for n, system in enumerate(systems):
            top, bottom = system[k : k + 1, :], system[k + 1 : k + 2, :]
            left, right = system[:, k : k + 1], system[:, k + 1 : k + 2]
            one, off, two = left[k : k + 1], right[k : k + 1], right[k + 1 : k + 2]
            scale = 1.0 / (one * two - off * off)
            upper = (two * top - off * bottom) * scale
            lower = (one * bottom - off * top) * scale
            rest = system - left * upper - right * lower
            systems[n] = jnp.where(first, upper, jnp.where(second, lower, rest))
    return [system[:, PAD:] for system in systems]


def identity():
    down, across = places()
    return jnp.where(down == across, 1.0, 0.0)


def pieces_of(array, count=3):
    pieces = []
    for _ in range(count):
        piece = array.astype(bf16)
        pieces.append(piece)
        array = array - piece.astype(f32)
    return pieces


def bdot(left, right, right_dim=0):
    return lax.dot_general(left, right, (((1,), (right_dim,)), ((), ())), preferred_element_type=f32)


def left_pieces(array):
    high, mid, low = pieces_of(array)
    return jnp.concatenate([high, high, high, mid, mid, low], 1)


def right_pieces(array, dim):
    high, mid, low = pieces_of(array)
    return jnp.concatenate([high, mid, low, high, mid, high], dim)


def wide_dot(left, right, right_dim=0):
    return bdot(left_pieces(left), right_pieces(right, right_dim), right_dim)


def tile_dot(tile_ref, right):
    first, second, third = pieces_of(right)
    both = jnp.concatenate([first, second], 1)
    by_high = bdot(tile_ref[0], jnp.concatenate([both, third], 1))
    by_mid = bdot(tile_ref[1], both)
    by_low = bdot(tile_ref[2], first)
    small = by_high[:, 2 * PAD :] + by_mid[:, PAD:] + by_low
    return by_high[:, :PAD] + (by_high[:, PAD : 2 * PAD] + by_mid[:, :PAD] + small)


def start_kernel(joined_ref, own_ref, col_ref):
    scaled = joined_ref[0:32, :FEAT] / joined_ref[63:64, :FEAT]
    down, _ = places()
    rhs = jnp.where(down < COLS, joined_ref[32:64, :PAD], 0.0).T
    pairs = [jnp.concatenate([scaled[16 * g : 16 * g + 8], scaled[16 * g + 8 : 16 * g + 16]], 1) for g in range(2)]
    block = jnp.concatenate(pairs + [pack(rhs)], 0)
    own_ref[...] = block
    col_ref[...] = jnp.broadcast_to(block[None], col_ref.shape)


def variances_of(joined_ref):
    return joined_ref[63:64, FEAT : FEAT + 1], joined_ref[63:64, FEAT + 1 : FEAT + 2]


def norm_lanes(points, first):
    across = lax.broadcasted_iota(jnp.int32, (points.shape[0], 128), 1)
    lanes = jnp.where((across >= 3 - first) & (across < 6 - first), 1.0, 0.0)
    for n, piece in enumerate(pieces_of(jnp.sum(points * points, 1, keepdims=True))):
        lanes = jnp.where(across == first + n, piece.astype(f32), lanes)
    return lanes.astype(bf16)


def tile_kernel(row_ref, col_ref, own_ref, tile_hbm, message_ref, work_ref, tile_ref, sems):
    row_points = unpack_points(row_ref) * root_five
    col_points = unpack_points(col_ref) * root_five
    left = jnp.concatenate([left_pieces(row_points), norm_lanes(row_points, 0)], 1)
    right = jnp.concatenate([right_pieces(-2.0 * col_points, 1), norm_lanes(col_points, 3)], 1)
    work_ref[...] = bdot(left, right, 1)

    def strip(i, carry):
        here = pl.ds(pl.multiple_of(i * 16, 16), 16)
        squared = jnp.maximum(work_ref[here, :], 0.0)
        dist = squared * lax.rsqrt(jnp.maximum(squared, 1e-30))
        decayed = jnp.exp(-dist)
        more = 1.0 + dist
        pieces = pieces_of((more + squared * (1.0 / 3.0)) * decayed) + pieces_of(more * decayed, 2)
        for n, piece in enumerate(pieces):
            tile_ref[n, here, :] = piece
        return carry

    rows = work_ref.shape[0]
    part = rows // PARTS
    copies = []
    for n in range(PARTS):
        lax.fori_loop(n * (part // 16), (n + 1) * (part // 16), strip, 0)
        here = pl.ds(n * part, part)
        copies.append(pltpu.make_async_copy(tile_ref.at[:, here, :], tile_hbm.at[:, here, :], sems.at[n]))
        copies[n].start()
    row_rhs = unpack_columns(row_ref, 16)
    col_rhs = unpack_columns(col_ref, 16)
    own_rhs = unpack(own_ref[16:24, :])
    partial = tile_dot(tile_ref, col_rhs)
    curvature = dot(row_rhs, partial, 0, 0)
    gram = dot(own_rhs, own_rhs, 0, 0)
    quarter = rows // 4
    chunks = jnp.concatenate([partial[quarter * g : quarter * g + quarter] for g in range(4)], 1)
    message_ref[:, 0:8, :] = chunks.reshape(quarter // 8, 8, 128)
    grams = pack(join_symmetric(symmetric(curvature), gram))
    message_ref[:, 8:16, :] = jnp.broadcast_to(grams[None], (quarter // 8, 8, 128))
    for copy in copies:
        copy.wait()


def images_kernel(got_ref, own_ref, joined_ref, own_images_ref, row_ref, col_ref):
    signal_var, noise_var = variances_of(joined_ref)
    summed = jnp.sum(got_ref[...], 0)
    images = signal_var * summed[0:8] + noise_var * own_ref[16:24, :]
    own_images_ref[...] = images
    row_ref[...] = jnp.broadcast_to(images[None], row_ref.shape)
    col_ref[...] = jnp.broadcast_to(jnp.concatenate([images, summed[8:16]], 0)[None], col_ref.shape)


def residual_of(rhs, images, advance):
    return rhs - wide_dot(images, advance)


def advance_kernel(got_ref, col_ref, joined_ref, tile_hbm, coef_ref, product_ref, tile_ref, sems):
    copy = pltpu.make_async_copy(tile_hbm.at[0:3], tile_ref, sems.at[0])
    copy.start()
    signal_var, noise_var = variances_of(joined_ref)
    base_curvature, res_gram = part_symmetric(unpack(jnp.sum(got_ref[:, 8:16, :], 0)))
    curvature = signal_var * base_curvature + noise_var * res_gram
    advance, inverse = eliminate(
        [jnp.concatenate([curvature, res_gram], 1), jnp.concatenate([res_gram, identity()], 1)]
    )
    residual = residual_of(unpack_columns(col_ref, 16), unpack_columns(got_ref, 0), advance)
    copy.wait()
    product_ref[...] = tile_dot(tile_ref, residual)
    middle = dot(inverse, dot(curvature, inverse))
    coef_ref[...] = jnp.concatenate([advance, inverse, symmetric(middle), jnp.zeros((PAD, PAD), f32)], 1)


def grams_kernel(got_ref, row_ref, own_ref, own_images_ref, coef_ref, product_ref, message_ref):
    advance = coef_ref[:, :PAD]
    residual = residual_of(unpack_columns(row_ref, 16), unpack_columns(got_ref, 0), advance)
    own_res = residual_of(unpack(own_ref[16:24, :]), unpack(own_images_ref[...]), advance)
    curvature = dot(residual, product_ref[...], 0, 0)
    gram = dot(own_res, own_res, 0, 0)
    message = pack(join_symmetric(symmetric(curvature), gram))
    message_ref[...] = jnp.broadcast_to(message[None], message_ref.shape)


def prepare_kernel(row_ref, col_ref, row_images_ref, col_images_ref, left_ref, right_ref, points_ref, moments_ref):
    left_ref[...] = left_pieces(jnp.concatenate([unpack_columns(row_ref, 16), unpack_columns(row_images_ref, 0)], 1))
    right = jnp.concatenate([unpack_columns(col_ref, 16), unpack_columns(col_images_ref, 0)], 1)
    right_ref[...] = right_pieces(right, 1)
    points_ref[...] = unpack_points(row_ref)
    col_points = unpack_points(col_ref)
    moments = pieces_of(jnp.concatenate([col_points, col_points * col_points], 1), 2)
    moments_ref[...] = jnp.concatenate(moments, 1)


def spread_kernel(got_ref, out_ref):
    out_ref[...] = jnp.broadcast_to(jnp.sum(got_ref[...], 0)[None], out_ref.shape)


def gradient_kernel(
    total_points,
    got_ref,
    coef_ref,
    own_ref,
    own_images_ref,
    joined_ref,
    left_ref,
    right_ref,
    points_ref,
    moments_ref,
    tile_hbm,
    solves_ref,
    terms_ref,
    tile_ref,
    matrix_ref,
    weighted_ref,
    sums_ref,
    sems,
):
    copies = []
    for n, k in enumerate((0, 1, 3, 4)):
        copies.append(pltpu.make_async_copy(tile_hbm.at[k], tile_ref.at[n], sems.at[n]))
        copies[n].start()
    signal_var, noise_var = variances_of(joined_ref)
    advance, inverse, middle = (coef_ref[:, PAD * g : PAD * g + PAD] for g in range(3))
    base_curvature, next_gram = part_symmetric(unpack(jnp.sum(got_ref[...], 0)))
    next_curv = signal_var * base_curvature + noise_var * next_gram - symmetric(dot(dot(next_gram, middle), next_gram))
    carry_over = dot(inverse, next_gram)
    (next_advance,) = eliminate([jnp.concatenate([next_curv, next_gram], 1)])
    coef = wide_dot(jnp.concatenate([identity() + carry_over, -advance], 0), next_advance)
    coef = coef + jnp.concatenate([advance, jnp.zeros((PAD, PAD), f32)], 0)
    _, across = places(2 * PAD, PAD)
    weights = jnp.where(across < PROBES, -1.0 / PROBES, 1.0) * (0.5 / total_points)
    target = jnp.where(across == PROBES, coef, 0.0)
    form = dot(target * (0.5 / total_points), target, 1, 1)
    probes = jnp.where(across < PROBES, coef * weights, 0.0)
    form = form + jnp.concatenate([probes, jnp.zeros((2 * PAD, PAD), f32)], 1)
    left = bdot(left_ref[...], right_pieces(form, 0))
    matrix_ref[...] = bdot(left_pieces(left), right_ref[...], 1)

    own_rhs = unpack(own_ref[16:24, :])
    own_solves = dot(jnp.concatenate([own_rhs, unpack(own_images_ref[...])], 1), coef)
    solves_ref[...] = own_solves.T[0:COLS, :]
    pair = jnp.where(across[:PAD] < PROBES, own_rhs, own_solves)
    noise = jnp.sum(own_solves * weights[:PAD] * pair, 0, keepdims=True)
    noise_term = noise_var * jnp.sum(noise, 1, keepdims=True)
    for copy in copies:
        copy.wait()

    def strip(i, total):
        here = pl.ds(pl.multiple_of(i * 16, 16), 16)
        values = matrix_ref[here, :]
        high, mid, slope_high, slope_low = (tile_ref[n, here, :].astype(f32) for n in range(4))
        weighted = values * (slope_high + slope_low)
        upper = weighted.astype(bf16)
        weighted_ref[0, here, :] = upper
        weighted_ref[1, here, :] = (weighted - upper.astype(f32)).astype(bf16)
        sums_ref[here, :] = jnp.broadcast_to(jnp.sum(weighted, 1, keepdims=True), (16, 128))
        return total + values * (high + mid)

    signal = lax.fori_loop(0, matrix_ref.shape[0] // 16, strip, jnp.zeros((16, matrix_ref.shape[1]), f32))
    by_upper = bdot(weighted_ref[0], moments_ref[...])
    moved = by_upper[:, :128] + (by_upper[:, 128:] + bdot(weighted_ref[1], moments_ref[:, :128]))
    points = points_ref[...]
    scales = points * (points * sums_ref[:, :FEAT] - 2.0 * moved[:, :FEAT]) + moved[:, FEAT:128]
    scale_terms = (5.0 / 3.0 * signal_var) * jnp.sum(scales, 0, keepdims=True)
    signal_term = signal_var * jnp.sum(jnp.sum(signal, 0, keepdims=True), 1, keepdims=True)
    terms_ref[...] = jnp.concatenate([scale_terms, signal_term, noise_term, jnp.zeros((1, FEAT - 2), f32)], 1)


def shape_of(*dims, dtype=f32):
    return jax.ShapeDtypeStruct(dims, dtype)


def call(kernel, outs, *operands, far_in=0, far_outs=0, scratch=(), flops=1):
    near, far = (pl.BlockSpec(memory_space=m) for m in (pltpu.VMEM, pltpu.HBM))
    return pl.pallas_call(
        kernel,
        out_shape=outs,
        in_specs=[near] * (len(operands) - far_in) + [far] * far_in,
        out_specs=[far] * far_outs + [near] * (len(outs) - far_outs),
        scratch_shapes=scratch,
        compiler_params=PARAMS,
        cost_estimate=pl.CostEstimate(flops=flops, bytes_accessed=1 << 20, transcendentals=0),
    )(*operands)


def exchange(blocks, axis):
    return lax.all_to_all(blocks, axis, 0, 0, tiled=True)


def local(points, length_scales, variances, targets, probe_vectors):
    rows = lax.axis_size("row")
    cols = lax.axis_size("col")
    width = points.shape[1]
    row_block, col_set = cols * width, rows * width
    total_points = width * rows * cols
    tile = (row_block, col_set)
    sems = pltpu.SemaphoreType.DMA((4,))

    def widen(array):
        return jnp.pad(array, ((0, 0), (0, 128 - array.shape[1])))

    scalars = jnp.concatenate([length_scales, variances])
    joined = jnp.concatenate([widen(a) for a in (points.T, probe_vectors, targets[None], scalars[None])], 0)
    own, to_col = call(start_kernel, [shape_of(24, 128), shape_of(rows, 24, 128)], joined)
    col_got = exchange(to_col, "row")
    row_got = lax.all_gather(own, "col")
    stack, message = call(
        tile_kernel,
        [shape_of(5, *tile, dtype=bf16), shape_of(cols, 16, 128)],
        row_got,
        col_got,
        own,
        far_outs=1,
        scratch=[pltpu.VMEM(tile, f32), pltpu.VMEM((5,) + tile, bf16), sems],
    )
    own_images, images_row, images_col = call(
        images_kernel,
        [shape_of(8, 128), shape_of(cols, 8, 128), shape_of(rows, 16, 128)],
        exchange(message, "col"),
        own,
        joined,
    )
    col_images = exchange(images_col, "row")
    row_images = exchange(images_row, "col")
    coef, product = call(
        advance_kernel,
        [shape_of(PAD, 128), shape_of(row_block, PAD)],
        col_images,
        col_got,
        joined,
        stack,
        far_in=1,
        scratch=[pltpu.VMEM((3,) + tile, bf16), sems],
    )
    (message,) = call(
        grams_kernel, [shape_of(cols, 8, 128)], row_images, row_got, own, own_images, coef, product
    )
    prepared = call(
        prepare_kernel,
        [
            shape_of(row_block, 12 * PAD, dtype=bf16),
            shape_of(col_set, 12 * PAD, dtype=bf16),
            shape_of(row_block, FEAT),
            shape_of(col_set, 4 * FEAT, dtype=bf16),
        ],
        row_got,
        col_got,
        row_images,
        col_images,
    )
    (message,) = call(spread_kernel, [shape_of(rows, 8, 128)], exchange(message, "col"))
    solves, terms = call(
        functools.partial(gradient_kernel, total_points),
        [shape_of(COLS, width), shape_of(1, 128)],
        exchange(message, "row"),
        coef,
        own,
        own_images,
        joined,
        *prepared,
        stack,
        far_in=1,
        scratch=[
            pltpu.VMEM((4,) + tile, bf16),
            pltpu.VMEM(tile, f32),
            pltpu.VMEM((2,) + tile, bf16),
            pltpu.VMEM((row_block, 128), f32),
            sems,
        ],
    )
    terms = jnp.sum(exchange(jnp.broadcast_to(terms[None], (cols, 1, 128)), "col"), 0)
    terms = jnp.sum(exchange(jnp.broadcast_to(terms[None], (rows, 1, 128)), "row"), 0)
    return (solves, terms[0, : FEAT + 2])


def solution(mesh):
    placed = (P(None, ("row", "col")), P(), P(), P(("row", "col")), P(None, ("row", "col")))
    return jax.shard_map(
        local, mesh=mesh, in_specs=placed, out_specs=(P(None, ("row", "col")), P()), check_vma=False
    )
```

```python
import functools

import jax
import jax.numpy as jnp
from jax import lax
from jax.experimental import pallas as pl
from jax.experimental.pallas import tpu as pltpu
from jax.sharding import PartitionSpec as P

PROBES = 30
COLS = 31
FEAT = 64
PAD = 32
PARTS = 4
f32 = jnp.float32
bf16 = jnp.bfloat16
root_five = 5.0**0.5
highest = lax.Precision.HIGHEST
NEAR, LARGE = 16 * 1024 * 1024, 50 * 1024 * 1024


def dot(left, right, left_dim=1, right_dim=0):
    return lax.dot_general(
        left, right, (((left_dim,), (right_dim,)), ((), ())), precision=highest, preferred_element_type=f32
    )


def pack(square):
    return jnp.concatenate([square[8 * g : 8 * g + 8] for g in range(4)], 1)


def unpack(rows):
    return jnp.concatenate([rows[:, PAD * g : PAD * g + PAD] for g in range(4)], 0)


def unpack_columns(ref, start):
    count = ref.shape[0]
    pieces = [ref[:, start : start + 8, PAD * g : PAD * g + PAD].reshape(8 * count, PAD) for g in range(4)]
    return jnp.concatenate(pieces, 0)


def unpack_points(ref):
    count = ref.shape[0]
    pieces = []
    for g in range(4):
        top, left = 8 * (g // 2), FEAT * (g % 2)
        pieces.append(ref[:, top : top + 8, left : left + FEAT].reshape(8 * count, FEAT))
    return jnp.concatenate(pieces, 0)


def places(rows=PAD, columns=PAD):
    shape = (rows, columns)
    return lax.broadcasted_iota(jnp.int32, shape, 0), lax.broadcasted_iota(jnp.int32, shape, 1)


def symmetric(matrix):
    return 0.5 * (matrix + matrix.T)


def join_symmetric(first, second):
    down, across = places()
    diagonal = jnp.sum(jnp.where(down == across, second, 0.0), 0, keepdims=True)
    return jnp.where(down == PAD - 1, diagonal, jnp.where(down >= across, first, second))


def part_symmetric(joined):
    down, across = places()
    inside = down < PAD - 1
    lower = jnp.where((down >= across) & inside, joined, 0.0)
    upper = jnp.where(down < across, joined, 0.0)
    eye = down == across
    first = jnp.where(eye, lower, lower + lower.T)
    second = upper + upper.T + jnp.where(eye, joined[PAD - 1 : PAD, :], 0.0)
    return first, second


def eliminate(systems):
    down, across = places(PAD, 2 * PAD)
    systems = [jnp.where((down == PAD - 1) & (across == PAD - 1), 1.0, system) for system in systems]
    for k in range(0, PAD, 2):
        first, second = down == k, down == k + 1
        for n, system in enumerate(systems):
            top, bottom = system[k : k + 1, :], system[k + 1 : k + 2, :]
            left, right = system[:, k : k + 1], system[:, k + 1 : k + 2]
            one, off, two = left[k : k + 1], right[k : k + 1], right[k + 1 : k + 2]
            scale = 1.0 / (one * two - off * off)
            upper = (two * top - off * bottom) * scale
            lower = (one * bottom - off * top) * scale
            rest = system - left * upper - right * lower
            systems[n] = jnp.where(first, upper, jnp.where(second, lower, rest))
    return [system[:, PAD:] for system in systems]


def identity():
    down, across = places()
    return jnp.where(down == across, 1.0, 0.0)


def pieces_of(array, count=3):
    pieces = []
    for _ in range(count):
        piece = array.astype(bf16)
        pieces.append(piece)
        array = array - piece.astype(f32)
    return pieces


def bdot(left, right, right_dim=0):
    return lax.dot_general(left, right, (((1,), (right_dim,)), ((), ())), preferred_element_type=f32)


def left_pieces(array):
    high, mid, low = pieces_of(array)
    return jnp.concatenate([high, high, high, mid, mid, low], 1)


def right_pieces(array, dim):
    high, mid, low = pieces_of(array)
    return jnp.concatenate([high, mid, low, high, mid, high], dim)


def wide_dot(left, right, right_dim=0):
    return bdot(left_pieces(left), right_pieces(right, right_dim), right_dim)


def tile_dot(tile_ref, right):
    first, second, third = pieces_of(right)
    both = jnp.concatenate([first, second], 1)
    by_high = bdot(tile_ref[0], jnp.concatenate([both, third], 1))
    by_mid = bdot(tile_ref[1], both)
    by_low = bdot(tile_ref[2], first)
    small = by_high[:, 2 * PAD :] + by_mid[:, PAD:] + by_low
    return by_high[:, :PAD] + (by_high[:, PAD : 2 * PAD] + by_mid[:, :PAD] + small)


def start_kernel(joined_ref, own_ref, col_ref):
    scaled = joined_ref[0:32, :FEAT] / joined_ref[63:64, :FEAT]
    down, _ = places()
    rhs = jnp.where(down < COLS, joined_ref[32:64, :PAD], 0.0).T
    pairs = [jnp.concatenate([scaled[16 * g : 16 * g + 8], scaled[16 * g + 8 : 16 * g + 16]], 1) for g in range(2)]
    block = jnp.concatenate(pairs + [pack(rhs)], 0)
    own_ref[...] = block
    col_ref[...] = jnp.broadcast_to(block[None], col_ref.shape)


def variances_of(joined_ref):
    return joined_ref[64:65, 0:1], joined_ref[64:65, 1:2]


def norm_lanes(points, first):
    across = lax.broadcasted_iota(jnp.int32, (points.shape[0], 128), 1)
    lanes = jnp.where((across >= 3 - first) & (across < 6 - first), 1.0, 0.0)
    for n, piece in enumerate(pieces_of(jnp.sum(points * points, 1, keepdims=True))):
        lanes = jnp.where(across == first + n, piece.astype(f32), lanes)
    return lanes.astype(bf16)


def tile_kernel(row_ref, col_ref, own_ref, tile_hbm, message_ref, work_ref, tile_ref, sems):
    row_points = unpack_points(row_ref) * root_five
    col_points = unpack_points(col_ref) * root_five
    left = jnp.concatenate([left_pieces(row_points), norm_lanes(row_points, 0)], 1)
    right = jnp.concatenate([right_pieces(-2.0 * col_points, 1), norm_lanes(col_points, 3)], 1)
    work_ref[...] = bdot(left, right, 1)

    def strip(i, carry):
        here = pl.ds(pl.multiple_of(i * 16, 16), 16)
        squared = jnp.maximum(work_ref[here, :], 0.0)
        dist = squared * lax.rsqrt(jnp.maximum(squared, 1e-30))
        decayed = jnp.exp(-dist)
        more = 1.0 + dist
        pieces = pieces_of((more + squared * (1.0 / 3.0)) * decayed) + pieces_of(more * decayed, 2)
        for n, piece in enumerate(pieces):
            tile_ref[n, here, :] = piece
        return carry

    rows = work_ref.shape[0]
    part = rows // PARTS
    copies = []
    for n in range(PARTS):
        lax.fori_loop(n * (part // 16), (n + 1) * (part // 16), strip, 0)
        here = pl.ds(n * part, part)
        copies.append(pltpu.make_async_copy(tile_ref.at[:, here, :], tile_hbm.at[:, here, :], sems.at[n]))
        copies[n].start()
    row_rhs = unpack_columns(row_ref, 16)
    col_rhs = unpack_columns(col_ref, 16)
    own_rhs = unpack(own_ref[16:24, :])
    partial = tile_dot(tile_ref, col_rhs)
    curvature = dot(row_rhs, partial, 0, 0)
    gram = dot(own_rhs, own_rhs, 0, 0)
    quarter = rows // 4
    chunks = jnp.concatenate([partial[quarter * g : quarter * g + quarter] for g in range(4)], 1)
    message_ref[:, 0:8, :] = chunks.reshape(quarter // 8, 8, 128)
    grams = pack(join_symmetric(symmetric(curvature), gram))
    message_ref[:, 8:16, :] = jnp.broadcast_to(grams[None], (quarter // 8, 8, 128))
    for copy in copies:
        copy.wait()


def images_kernel(got_ref, own_ref, joined_ref, own_images_ref, row_ref, col_ref):
    signal_var, noise_var = variances_of(joined_ref)
    summed = jnp.sum(got_ref[...], 0)
    images = signal_var * summed[0:8] + noise_var * own_ref[16:24, :]
    own_images_ref[...] = images
    row_ref[...] = jnp.broadcast_to(images[None], row_ref.shape)
    col_ref[...] = jnp.broadcast_to(jnp.concatenate([images, summed[8:16]], 0)[None], col_ref.shape)


def residual_of(rhs, images, advance):
    return rhs - wide_dot(images, advance)


def advance_kernel(got_ref, col_ref, joined_ref, tile_hbm, coef_ref, product_ref, tile_ref, sems):
    copy = pltpu.make_async_copy(tile_hbm.at[0:3], tile_ref, sems.at[0])
    copy.start()
    signal_var, noise_var = variances_of(joined_ref)
    base_curvature, res_gram = part_symmetric(unpack(jnp.sum(got_ref[:, 8:16, :], 0)))
    curvature = signal_var * base_curvature + noise_var * res_gram
    advance, inverse = eliminate(
        [jnp.concatenate([curvature, res_gram], 1), jnp.concatenate([res_gram, identity()], 1)]
    )
    residual = residual_of(unpack_columns(col_ref, 16), unpack_columns(got_ref, 0), advance)
    copy.wait()
    product_ref[...] = tile_dot(tile_ref, residual)
    middle = dot(inverse, dot(curvature, inverse))
    coef_ref[...] = jnp.concatenate([advance, inverse, symmetric(middle), jnp.zeros((PAD, PAD), f32)], 1)


def grams_kernel(got_ref, row_ref, own_ref, own_images_ref, coef_ref, product_ref, message_ref):
    advance = coef_ref[:, :PAD]
    residual = residual_of(unpack_columns(row_ref, 16), unpack_columns(got_ref, 0), advance)
    own_res = residual_of(unpack(own_ref[16:24, :]), unpack(own_images_ref[...]), advance)
    curvature = dot(residual, product_ref[...], 0, 0)
    gram = dot(own_res, own_res, 0, 0)
    message = pack(join_symmetric(symmetric(curvature), gram))
    message_ref[...] = jnp.broadcast_to(message[None], message_ref.shape)


def prepare_kernel(row_ref, col_ref, row_images_ref, col_images_ref, left_ref, right_ref, points_ref, moments_ref):
    left_ref[...] = left_pieces(jnp.concatenate([unpack_columns(row_ref, 16), unpack_columns(row_images_ref, 0)], 1))
    right = jnp.concatenate([unpack_columns(col_ref, 16), unpack_columns(col_images_ref, 0)], 1)
    right_ref[...] = right_pieces(right, 1)
    points_ref[...] = unpack_points(row_ref)
    col_points = unpack_points(col_ref)
    moments = pieces_of(jnp.concatenate([col_points, col_points * col_points], 1), 2)
    moments_ref[...] = jnp.concatenate(moments, 1)


def spread_kernel(got_ref, out_ref):
    out_ref[...] = jnp.broadcast_to(jnp.sum(got_ref[...], 0)[None], out_ref.shape)


def gradient_kernel(
    total_points,
    got_ref,
    coef_ref,
    own_ref,
    own_images_ref,
    joined_ref,
    left_ref,
    right_ref,
    points_ref,
    moments_ref,
    tile_hbm,
    solves_ref,
    terms_ref,
    tile_ref,
    matrix_ref,
    weighted_ref,
    sums_ref,
    sems,
):
    copies = []
    for n, k in enumerate((0, 1, 3, 4)):
        copies.append(pltpu.make_async_copy(tile_hbm.at[k], tile_ref.at[n], sems.at[n]))
        copies[n].start()
    signal_var, noise_var = variances_of(joined_ref)
    advance, inverse, middle = (coef_ref[:, PAD * g : PAD * g + PAD] for g in range(3))
    base_curvature, next_gram = part_symmetric(unpack(jnp.sum(got_ref[...], 0)))
    next_curv = signal_var * base_curvature + noise_var * next_gram - symmetric(dot(dot(next_gram, middle), next_gram))
    carry_over = dot(inverse, next_gram)
    (next_advance,) = eliminate([jnp.concatenate([next_curv, next_gram], 1)])
    coef = wide_dot(jnp.concatenate([identity() + carry_over, -advance], 0), next_advance)
    coef = coef + jnp.concatenate([advance, jnp.zeros((PAD, PAD), f32)], 0)
    _, across = places(2 * PAD, PAD)
    weights = jnp.where(across < PROBES, -1.0 / PROBES, 1.0) * (0.5 / total_points)
    target = jnp.where(across == PROBES, coef, 0.0)
    form = dot(target * (0.5 / total_points), target, 1, 1)
    probes = jnp.where(across < PROBES, coef * weights, 0.0)
    form = form + jnp.concatenate([probes, jnp.zeros((2 * PAD, PAD), f32)], 1)
    left = bdot(left_ref[...], right_pieces(form, 0))
    matrix_ref[...] = bdot(left_pieces(left), right_ref[...], 1)

    own_rhs = unpack(own_ref[16:24, :])
    own_solves = dot(jnp.concatenate([own_rhs, unpack(own_images_ref[...])], 1), coef)
    solves_ref[...] = own_solves.T[0:COLS, :]
    pair = jnp.where(across[:PAD] < PROBES, own_rhs, own_solves)
    noise = jnp.sum(own_solves * weights[:PAD] * pair, 0, keepdims=True)
    noise_term = noise_var * jnp.sum(noise, 1, keepdims=True)
    for copy in copies:
        copy.wait()

    def strip(i, total):
        here = pl.ds(pl.multiple_of(i * 16, 16), 16)
        values = matrix_ref[here, :]
        high, mid, slope_high, slope_low = (tile_ref[n, here, :].astype(f32) for n in range(4))
        weighted = values * (slope_high + slope_low)
        upper = weighted.astype(bf16)
        weighted_ref[0, here, :] = upper
        weighted_ref[1, here, :] = (weighted - upper.astype(f32)).astype(bf16)
        sums_ref[here, :] = jnp.broadcast_to(jnp.sum(weighted, 1, keepdims=True), (16, 128))
        return total + values * (high + mid)

    signal = lax.fori_loop(0, matrix_ref.shape[0] // 16, strip, jnp.zeros((16, matrix_ref.shape[1]), f32))
    by_upper = bdot(weighted_ref[0], moments_ref[...])
    moved = by_upper[:, :128] + (by_upper[:, 128:] + bdot(weighted_ref[1], moments_ref[:, :128]))
    points = points_ref[...]
    scales = points * (points * sums_ref[:, :FEAT] - 2.0 * moved[:, :FEAT]) + moved[:, FEAT:128]
    scale_terms = (5.0 / 3.0 * signal_var) * jnp.sum(scales, 0, keepdims=True)
    signal_term = signal_var * jnp.sum(jnp.sum(signal, 0, keepdims=True), 1, keepdims=True)
    terms_ref[...] = jnp.concatenate([scale_terms, signal_term, noise_term, jnp.zeros((1, FEAT - 2), f32)], 1)


def shape_of(*dims, dtype=f32):
    return jax.ShapeDtypeStruct(dims, dtype)


def call(kernel, outs, *operands, far_in=0, far_outs=0, scratch=(), limit=NEAR):
    near, far = (pl.BlockSpec(memory_space=m) for m in (pltpu.VMEM, pltpu.HBM))
    return pl.pallas_call(
        kernel,
        out_shape=outs,
        in_specs=[near] * (len(operands) - far_in) + [far] * far_in,
        out_specs=[far] * far_outs + [near] * (len(outs) - far_outs),
        scratch_shapes=scratch,
        compiler_params=pltpu.CompilerParams(vmem_limit_bytes=limit),
        cost_estimate=pl.CostEstimate(flops=1, bytes_accessed=1 << 20, transcendentals=0),
    )(*operands)


def exchange(blocks, axis):
    return lax.all_to_all(blocks, axis, 0, 0, tiled=True)


def local(points, length_scales, variances, targets, probe_vectors):
    rows = lax.axis_size("row")
    cols = lax.axis_size("col")
    width = points.shape[1]
    row_block, col_set = cols * width, rows * width
    total_points = width * rows * cols
    tile = (row_block, col_set)
    sems = pltpu.SemaphoreType.DMA((4,))

    def widen(array):
        return jnp.pad(array, ((0, 0), (0, 128 - array.shape[1])))

    parts = (points.T, probe_vectors, targets[None], length_scales[None], variances[None])
    joined = jnp.concatenate([widen(a) for a in parts], 0)
    own, to_col = call(start_kernel, [shape_of(24, 128), shape_of(rows, 24, 128)], joined)
    col_got = exchange(to_col, "row")
    row_got = lax.all_gather(own, "col")
    stack, message = call(
        tile_kernel,
        [shape_of(5, *tile, dtype=bf16), shape_of(cols, 16, 128)],
        row_got,
        col_got,
        own,
        far_outs=1,
        limit=LARGE,
        scratch=[pltpu.VMEM(tile, f32), pltpu.VMEM((5,) + tile, bf16), sems],
    )
    own_images, images_row, images_col = call(
        images_kernel,
        [shape_of(8, 128), shape_of(cols, 8, 128), shape_of(rows, 16, 128)],
        exchange(message, "col"),
        own,
        joined,
    )
    col_images = exchange(images_col, "row")
    row_images = exchange(images_row, "col")
    coef, product = call(
        advance_kernel,
        [shape_of(PAD, 128), shape_of(row_block, PAD)],
        col_images,
        col_got,
        joined,
        stack,
        far_in=1,
        limit=LARGE,
        scratch=[pltpu.VMEM((3,) + tile, bf16), sems],
    )
    (message,) = call(
        grams_kernel, [shape_of(cols, 8, 128)], row_images, row_got, own, own_images, coef, product
    )
    prepared = call(
        prepare_kernel,
        [
            shape_of(row_block, 12 * PAD, dtype=bf16),
            shape_of(col_set, 12 * PAD, dtype=bf16),
            shape_of(row_block, FEAT),
            shape_of(col_set, 4 * FEAT, dtype=bf16),
        ],
        row_got,
        col_got,
        row_images,
        col_images,
    )
    (message,) = call(spread_kernel, [shape_of(rows, 8, 128)], exchange(message, "col"))
    solves, terms = call(
        functools.partial(gradient_kernel, total_points),
        [shape_of(COLS, width), shape_of(1, 128)],
        exchange(message, "row"),
        coef,
        own,
        own_images,
        joined,
        *prepared,
        stack,
        far_in=1,
        limit=LARGE,
        scratch=[
            pltpu.VMEM((4,) + tile, bf16),
            pltpu.VMEM(tile, f32),
            pltpu.VMEM((2,) + tile, bf16),
            pltpu.VMEM((row_block, 128), f32),
            sems,
        ],
    )
    terms = jnp.sum(exchange(jnp.broadcast_to(terms[None], (cols, 1, 128)), "col"), 0)
    terms = jnp.sum(exchange(jnp.broadcast_to(terms[None], (rows, 1, 128)), "row"), 0)
    return (solves, terms[0, : FEAT + 2])


def solution(mesh):
    placed = (P(None, ("row", "col")), P(), P(), P(("row", "col")), P(None, ("row", "col")))
    return jax.shard_map(
        local, mesh=mesh, in_specs=placed, out_specs=(P(None, ("row", "col")), P()), check_vma=False
    )
```

```python
import functools

import jax
import jax.numpy as jnp
from jax import lax
from jax.experimental import pallas as pl
from jax.experimental.pallas import tpu as pltpu
from jax.sharding import PartitionSpec as P

PROBES = 30
COLS = 31
FEAT = 64
PAD = 32
PARTS = 4
f32 = jnp.float32
bf16 = jnp.bfloat16
root_five = 5.0**0.5
highest = lax.Precision.HIGHEST
NEAR, LARGE, WHOLE = 16 * 1024 * 1024, 50 * 1024 * 1024, 60 * 1024 * 1024


def dot(left, right, left_dim=1, right_dim=0):
    return lax.dot_general(
        left, right, (((left_dim,), (right_dim,)), ((), ())), precision=highest, preferred_element_type=f32
    )


def pack(square):
    return jnp.concatenate([square[8 * g : 8 * g + 8] for g in range(4)], 1)


def unpack(rows):
    return jnp.concatenate([rows[:, PAD * g : PAD * g + PAD] for g in range(4)], 0)


def unpack_columns(ref, start):
    count = ref.shape[0]
    pieces = [ref[:, start : start + 8, PAD * g : PAD * g + PAD].reshape(8 * count, PAD) for g in range(4)]
    return jnp.concatenate(pieces, 0)


def unpack_points(ref):
    count = ref.shape[0]
    pieces = []
    for g in range(4):
        top, left = 8 * (g // 2), FEAT * (g % 2)
        pieces.append(ref[:, top : top + 8, left : left + FEAT].reshape(8 * count, FEAT))
    return jnp.concatenate(pieces, 0)


def places(rows=PAD, columns=PAD):
    shape = (rows, columns)
    return lax.broadcasted_iota(jnp.int32, shape, 0), lax.broadcasted_iota(jnp.int32, shape, 1)


def symmetric(matrix):
    return 0.5 * (matrix + matrix.T)


def join_symmetric(first, second):
    down, across = places()
    diagonal = jnp.sum(jnp.where(down == across, second, 0.0), 0, keepdims=True)
    return jnp.where(down == PAD - 1, diagonal, jnp.where(down >= across, first, second))


def part_symmetric(joined):
    down, across = places()
    inside = down < PAD - 1
    lower = jnp.where((down >= across) & inside, joined, 0.0)
    upper = jnp.where(down < across, joined, 0.0)
    eye = down == across
    first = jnp.where(eye, lower, lower + lower.T)
    second = upper + upper.T + jnp.where(eye, joined[PAD - 1 : PAD, :], 0.0)
    return first, second


def eliminate(systems):
    down, across = places(PAD, 2 * PAD)
    systems = [jnp.where((down == PAD - 1) & (across == PAD - 1), 1.0, system) for system in systems]
    for k in range(0, PAD, 2):
        first, second = down == k, down == k + 1
        for n, system in enumerate(systems):
            top, bottom = system[k : k + 1, :], system[k + 1 : k + 2, :]
            left, right = system[:, k : k + 1], system[:, k + 1 : k + 2]
            one, off, two = left[k : k + 1], right[k : k + 1], right[k + 1 : k + 2]
            scale = 1.0 / (one * two - off * off)
            upper = (two * top - off * bottom) * scale
            lower = (one * bottom - off * top) * scale
            rest = system - left * upper - right * lower
            systems[n] = jnp.where(first, upper, jnp.where(second, lower, rest))
    return [system[:, PAD:] for system in systems]


def identity():
    down, across = places()
    return jnp.where(down == across, 1.0, 0.0)


def pieces_of(array, count=3):
    pieces = []
    for _ in range(count):
        piece = array.astype(bf16)
        pieces.append(piece)
        array = array - piece.astype(f32)
    return pieces


def bdot(left, right, right_dim=0):
    return lax.dot_general(left, right, (((1,), (right_dim,)), ((), ())), preferred_element_type=f32)


def left_pieces(array):
    high, mid, low = pieces_of(array)
    return jnp.concatenate([high, high, high, mid, mid, low], 1)


def right_pieces(array, dim):
    high, mid, low = pieces_of(array)
    return jnp.concatenate([high, mid, low, high, mid, high], dim)


def wide_dot(left, right, right_dim=0):
    return bdot(left_pieces(left), right_pieces(right, right_dim), right_dim)


def tile_dot(tile_ref, right):
    first, second, third = pieces_of(right)
    both = jnp.concatenate([first, second], 1)
    by_high = bdot(tile_ref[0], jnp.concatenate([both, third], 1))
    by_mid = bdot(tile_ref[1], both)
    by_low = bdot(tile_ref[2], first)
    small = by_high[:, 2 * PAD :] + by_mid[:, PAD:] + by_low
    return by_high[:, :PAD] + (by_high[:, PAD : 2 * PAD] + by_mid[:, :PAD] + small)


def start_kernel(
    points_hbm, probes_hbm, targets_hbm, lengths_hbm, variances_hbm,
    own_ref, col_ref,
    points_ref, probes_ref, targets_ref, lengths_ref, variances_ref, sems,
):
    sources = (points_hbm, probes_hbm, targets_hbm, lengths_hbm, variances_hbm)
    targets = (points_ref, probes_ref, targets_ref, lengths_ref, variances_ref)
    copies = [pltpu.make_async_copy(a, b, sems.at[n]) for n, (a, b) in enumerate(zip(sources, targets))]
    for copy in copies:
        copy.start()
    for copy in copies:
        copy.wait()
    scaled = points_ref[...] / lengths_ref[...]
    rhs = jnp.concatenate([probes_ref[...], targets_ref[...], jnp.zeros((1, PAD), f32)], 0).T
    pairs = [jnp.concatenate([scaled[16 * g : 16 * g + 8], scaled[16 * g + 8 : 16 * g + 16]], 1) for g in range(2)]
    block = jnp.concatenate(pairs + [pack(rhs)], 0)
    scalars = jnp.concatenate([variances_ref[...], jnp.zeros((1, 126), f32)], 1)
    own_ref[...] = jnp.concatenate([block, jnp.broadcast_to(scalars, (8, 128))], 0)
    col_ref[...] = jnp.broadcast_to(block[None], col_ref.shape)


def variances_of(own_ref):
    return own_ref[8:9, 0:1], own_ref[8:9, 1:2]


def norm_lanes(points, first):
    squares = jnp.concatenate(pieces_of(points * points), 1)
    norms = bdot(squares, jnp.ones((squares.shape[1], 128), bf16))
    across = lax.broadcasted_iota(jnp.int32, norms.shape, 1)
    lanes = jnp.where((across >= 3 - first) & (across < 6 - first), 1.0, 0.0)
    for n, piece in enumerate(pieces_of(norms)):
        lanes = jnp.where(across == first + n, piece.astype(f32), lanes)
    return lanes.astype(bf16)


def tile_kernel(row_ref, col_ref, tile_hbm, message_ref, own_ref, work_ref, tile_ref, sems):
    own_ref[...] = row_ref[lax.axis_index("col"), 16:32, :]
    row_points = unpack_points(row_ref) * root_five
    col_points = unpack_points(col_ref) * root_five
    left = jnp.concatenate([left_pieces(row_points), norm_lanes(row_points, 0)], 1)
    right = jnp.concatenate([right_pieces(-2.0 * col_points, 1), norm_lanes(col_points, 3)], 1)
    work_ref[...] = bdot(left, right, 1)

    def strip(i, carry):
        here = pl.ds(pl.multiple_of(i * 16, 16), 16)
        squared = jnp.maximum(work_ref[here, :], 0.0)
        dist = squared * lax.rsqrt(jnp.maximum(squared, 1e-30))
        decayed = jnp.exp(-dist)
        more = 1.0 + dist
        pieces = pieces_of((more + squared * (1.0 / 3.0)) * decayed) + pieces_of(more * decayed, 2)
        for n, piece in enumerate(pieces):
            tile_ref[n, here, :] = piece
        return carry

    rows = work_ref.shape[0]
    part = rows // PARTS
    copies = []
    for n in range(PARTS):
        lax.fori_loop(n * (part // 16), (n + 1) * (part // 16), strip, 0)
        here = pl.ds(n * part, part)
        copies.append(pltpu.make_async_copy(tile_ref.at[:, here, :], tile_hbm.at[:, here, :], sems.at[n]))
        copies[n].start()
    row_rhs = unpack_columns(row_ref, 16)
    col_rhs = unpack_columns(col_ref, 16)
    own_rhs = unpack(own_ref[0:8, :])
    partial = tile_dot(tile_ref, col_rhs)
    curvature = dot(row_rhs, partial, 0, 0)
    gram = dot(own_rhs, own_rhs, 0, 0)
    quarter = rows // 4
    chunks = jnp.concatenate([partial[quarter * g : quarter * g + quarter] for g in range(4)], 1)
    message_ref[:, 0:8, :] = chunks.reshape(quarter // 8, 8, 128)
    grams = pack(join_symmetric(symmetric(curvature), gram))
    message_ref[:, 8:16, :] = jnp.broadcast_to(grams[None], (quarter // 8, 8, 128))
    for copy in copies:
        copy.wait()


def images_kernel(got_ref, own_ref, own_images_ref, row_ref, col_ref):
    signal_var, noise_var = variances_of(own_ref)
    summed = jnp.sum(got_ref[...], 0)
    images = signal_var * summed[0:8] + noise_var * own_ref[0:8, :]
    own_images_ref[...] = images
    row_ref[...] = jnp.broadcast_to(images[None], row_ref.shape)
    col_ref[...] = jnp.broadcast_to(jnp.concatenate([images, summed[8:16]], 0)[None], col_ref.shape)


def residual_of(rhs, images, advance):
    wide = jnp.concatenate([advance] * 4, 1)
    down, across = places(4 * PAD, 4 * PAD)
    repeated = jnp.where(down // PAD == across // PAD, jnp.concatenate([wide] * 4, 0), 0.0)
    return rhs - wide_dot(images, repeated)


def unpack_values(values):
    return jnp.concatenate([values[:, PAD * g : PAD * g + PAD] for g in range(4)], 0)


def packed_rows(ref, start):
    return ref[:, start : start + 8, :].reshape(8 * ref.shape[0], 128)


def advance_kernel(got_ref, col_ref, own_ref, tile_hbm, coef_ref, product_ref, tile_ref, sems):
    copy = pltpu.make_async_copy(tile_hbm.at[0:3], tile_ref, sems.at[0])
    copy.start()
    signal_var, noise_var = variances_of(own_ref)
    base_curvature, res_gram = part_symmetric(unpack(jnp.sum(got_ref[:, 8:16, :], 0)))
    curvature = signal_var * base_curvature + noise_var * res_gram
    advance, inverse = eliminate(
        [jnp.concatenate([curvature, res_gram], 1), jnp.concatenate([res_gram, identity()], 1)]
    )
    residual = unpack_values(residual_of(packed_rows(col_ref, 16), packed_rows(got_ref, 0), advance))
    copy.wait()
    product_ref[...] = tile_dot(tile_ref, residual)
    middle = dot(inverse, dot(curvature, inverse))
    coef_ref[...] = jnp.concatenate([advance, inverse, symmetric(middle), jnp.zeros((PAD, PAD), f32)], 1)


def grams_kernel(got_ref, row_ref, own_ref, own_images_ref, coef_ref, product_ref, message_ref):
    advance = coef_ref[:, :PAD]
    residual = unpack_values(residual_of(packed_rows(row_ref, 16), packed_rows(got_ref, 0), advance))
    own_res = unpack(residual_of(own_ref[0:8, :], own_images_ref[...], advance))
    curvature = dot(residual, product_ref[...], 0, 0)
    gram = dot(own_res, own_res, 0, 0)
    message = pack(join_symmetric(symmetric(curvature), gram))
    message_ref[...] = jnp.broadcast_to(message[None], message_ref.shape)


def prepare_kernel(row_ref, col_ref, row_images_ref, col_images_ref, left_ref, right_ref, points_ref, moments_ref):
    left_ref[...] = left_pieces(jnp.concatenate([unpack_columns(row_ref, 16), unpack_columns(row_images_ref, 0)], 1))
    right = jnp.concatenate([unpack_columns(col_ref, 16), unpack_columns(col_images_ref, 0)], 1)
    right_ref[...] = right_pieces(right, 1)
    points_ref[...] = unpack_points(row_ref)
    col_points = unpack_points(col_ref)
    moments = pieces_of(jnp.concatenate([col_points, col_points * col_points], 1), 2)
    moments_ref[...] = jnp.concatenate(moments, 1)


def spread_kernel(got_ref, out_ref):
    out_ref[...] = jnp.broadcast_to(jnp.sum(got_ref[...], 0)[None], out_ref.shape)


def gradient_kernel(
    total_points,
    got_ref,
    coef_ref,
    own_ref,
    own_images_ref,
    left_ref,
    right_ref,
    points_ref,
    moments_ref,
    tile_hbm,
    solves_ref,
    terms_ref,
    tile_ref,
    matrix_ref,
    weighted_ref,
    sums_ref,
    sems,
):
    copies = []
    for n, k in enumerate((0, 1, 3, 4)):
        copies.append(pltpu.make_async_copy(tile_hbm.at[k], tile_ref.at[n], sems.at[n]))
        copies[n].start()
    signal_var, noise_var = variances_of(own_ref)
    advance, inverse, middle = (coef_ref[:, PAD * g : PAD * g + PAD] for g in range(3))
    base_curvature, next_gram = part_symmetric(unpack(jnp.sum(got_ref[...], 0)))
    next_curv = signal_var * base_curvature + noise_var * next_gram - dot(dot(next_gram, middle), next_gram)
    carry_over = dot(inverse, next_gram)
    (next_advance,) = eliminate([jnp.concatenate([next_curv, next_gram], 1)])
    coef = wide_dot(jnp.concatenate([identity() + carry_over, -advance], 0), next_advance)
    coef = coef + jnp.concatenate([advance, jnp.zeros((PAD, PAD), f32)], 0)
    _, across = places(2 * PAD, PAD)
    weights = jnp.where(across < PROBES, -1.0 / PROBES, 1.0) * (0.5 / total_points)
    target = jnp.where(across == PROBES, coef, 0.0)
    form = dot(target * (0.5 / total_points), target, 1, 1)
    probes = jnp.where(across < PROBES, coef * weights, 0.0)
    form = form + jnp.concatenate([probes, jnp.zeros((2 * PAD, PAD), f32)], 1)
    left = bdot(left_ref[...], right_pieces(form, 0))
    matrix_ref[...] = bdot(left_pieces(left), right_ref[...], 1)

    own_rhs = unpack(own_ref[0:8, :])
    own_solves = dot(jnp.concatenate([own_rhs, unpack(own_images_ref[...])], 1), coef)
    solves_ref[...] = own_solves.T[0:COLS, :]
    pair = jnp.where(across[:PAD] < PROBES, own_rhs, own_solves)
    noise = jnp.sum(own_solves * weights[:PAD] * pair, 0, keepdims=True)
    noise_term = noise_var * jnp.sum(noise, 1, keepdims=True)
    for copy in copies:
        copy.wait()

    def strip(i, total):
        here = pl.ds(pl.multiple_of(i * 16, 16), 16)
        values = matrix_ref[here, :]
        high, mid, slope_high, slope_low = (tile_ref[n, here, :].astype(f32) for n in range(4))
        weighted = values * (slope_high + slope_low)
        upper = weighted.astype(bf16)
        weighted_ref[0, here, :] = upper
        weighted_ref[1, here, :] = (weighted - upper.astype(f32)).astype(bf16)
        sums_ref[here, :] = sum(weighted[:, 128 * g : 128 * g + 128] for g in range(weighted.shape[1] // 128))
        return total + values * (high + mid)

    signal = lax.fori_loop(0, matrix_ref.shape[0] // 16, strip, jnp.zeros((16, matrix_ref.shape[1]), f32))
    by_upper = bdot(weighted_ref[0], moments_ref[...])
    moved = by_upper[:, :128] + (by_upper[:, 128:] + bdot(weighted_ref[1], moments_ref[:, :128]))
    sums_high, sums_low = pieces_of(sums_ref[...], 2)
    ones = jnp.ones((128, 128), bf16)
    row_sums = bdot(sums_high, ones) + bdot(sums_low, ones)
    points = points_ref[...]
    scales = points * (points * row_sums[:, :FEAT] - 2.0 * moved[:, :FEAT]) + moved[:, FEAT:128]
    scale_terms = (5.0 / 3.0 * signal_var) * jnp.sum(scales, 0, keepdims=True)
    signal_term = signal_var * jnp.sum(jnp.sum(signal, 0, keepdims=True), 1, keepdims=True)
    terms_ref[...] = jnp.concatenate([scale_terms, signal_term, noise_term, jnp.zeros((1, FEAT - 2), f32)], 1)


def shape_of(*dims, dtype=f32):
    return jax.ShapeDtypeStruct(dims, dtype)


def call(kernel, outs, *operands, far_in=0, far_outs=0, scratch=(), limit=NEAR):
    near, far = (pl.BlockSpec(memory_space=m) for m in (pltpu.VMEM, pltpu.HBM))
    return pl.pallas_call(
        kernel,
        out_shape=outs,
        in_specs=[near] * (len(operands) - far_in) + [far] * far_in,
        out_specs=[far] * far_outs + [near] * (len(outs) - far_outs),
        scratch_shapes=scratch,
        compiler_params=pltpu.CompilerParams(vmem_limit_bytes=limit),
        cost_estimate=pl.CostEstimate(flops=1, bytes_accessed=1 << 20, transcendentals=0),
    )(*operands)


def exchange(blocks, axis):
    return lax.all_to_all(blocks, axis, 0, 0, tiled=True)


def local(points, length_scales, variances, targets, probe_vectors):
    rows = lax.axis_size("row")
    cols = lax.axis_size("col")
    width = points.shape[1]
    row_block, col_set = cols * width, rows * width
    total_points = width * rows * cols
    tile = (row_block, col_set)
    sems = pltpu.SemaphoreType.DMA((4,))

    to_row, to_col = call(
        start_kernel,
        [shape_of(32, 128), shape_of(rows, 24, 128)],
        points.T,
        probe_vectors,
        targets[None],
        length_scales[None],
        variances[None],
        far_in=5,
        limit=WHOLE,
        scratch=[
            pltpu.VMEM((width, FEAT), f32),
            pltpu.VMEM((PROBES, width), f32),
            pltpu.VMEM((1, width), f32),
            pltpu.VMEM((1, FEAT), f32),
            pltpu.VMEM((1, 2), f32),
            pltpu.SemaphoreType.DMA((5,)),
        ],
    )
    col_got = exchange(to_col, "row")
    row_got = lax.all_gather(to_row, "col")
    stack, message, own = call(
        tile_kernel,
        [shape_of(5, *tile, dtype=bf16), shape_of(cols, 16, 128), shape_of(16, 128)],
        row_got,
        col_got,
        far_outs=1,
        limit=LARGE,
        scratch=[pltpu.VMEM(tile, f32), pltpu.VMEM((5,) + tile, bf16), sems],
    )
    own_images, images_row, images_col = call(
        images_kernel,
        [shape_of(8, 128), shape_of(cols, 8, 128), shape_of(rows, 16, 128)],
        exchange(message, "col"),
        own,
    )
    col_images = exchange(images_col, "row")
    row_images = exchange(images_row, "col")
    coef, product = call(
        advance_kernel,
        [shape_of(PAD, 128), shape_of(row_block, PAD)],
        col_images,
        col_got,
        own,
        stack,
        far_in=1,
        limit=LARGE,
        scratch=[pltpu.VMEM((3,) + tile, bf16), sems],
    )
    (message,) = call(
        grams_kernel, [shape_of(cols, 8, 128)], row_images, row_got, own, own_images, coef, product
    )
    prepared = call(
        prepare_kernel,
        [
            shape_of(row_block, 12 * PAD, dtype=bf16),
            shape_of(col_set, 12 * PAD, dtype=bf16),
            shape_of(row_block, FEAT),
            shape_of(col_set, 4 * FEAT, dtype=bf16),
        ],
        row_got,
        col_got,
        row_images,
        col_images,
    )
    (message,) = call(spread_kernel, [shape_of(rows, 8, 128)], exchange(message, "col"))
    solves, terms = call(
        functools.partial(gradient_kernel, total_points),
        [shape_of(COLS, width), shape_of(1, 128)],
        exchange(message, "row"),
        coef,
        own,
        own_images,
        *prepared,
        stack,
        far_in=1,
        limit=LARGE,
        scratch=[
            pltpu.VMEM((4,) + tile, bf16),
            pltpu.VMEM(tile, f32),
            pltpu.VMEM((2,) + tile, bf16),
            pltpu.VMEM((row_block, 128), f32),
            sems,
        ],
    )
    terms = jnp.sum(exchange(jnp.broadcast_to(terms[None], (cols, 1, 128)), "col"), 0)
    terms = jnp.sum(exchange(jnp.broadcast_to(terms[None], (rows, 1, 128)), "row"), 0)
    return (solves, terms[0, : FEAT + 2])


def solution(mesh):
    placed = (P(None, ("row", "col")), P(), P(), P(("row", "col")), P(None, ("row", "col")))
    return jax.shard_map(
        local, mesh=mesh, in_specs=placed, out_specs=(P(None, ("row", "col")), P()), check_vma=False
    )
```

```python
import functools

import jax
import jax.numpy as jnp
from jax import lax
from jax.experimental import pallas as pl
from jax.experimental.pallas import tpu as pltpu
from jax.sharding import PartitionSpec as P

PROBES = 30
COLS = 31
FEAT = 64
PAD = 32
PARTS = 4
f32 = jnp.float32
bf16 = jnp.bfloat16
root_five = 5.0**0.5
highest = lax.Precision.HIGHEST
NEAR, LARGE, WHOLE = 16 * 1024 * 1024, 50 * 1024 * 1024, 60 * 1024 * 1024


def dot(left, right, left_dim=1, right_dim=0):
    return lax.dot_general(
        left, right, (((left_dim,), (right_dim,)), ((), ())), precision=highest, preferred_element_type=f32
    )


def pack(square):
    return jnp.concatenate([square[8 * g : 8 * g + 8] for g in range(4)], 1)


def unpack(rows):
    return jnp.concatenate([rows[:, PAD * g : PAD * g + PAD] for g in range(4)], 0)


def unpack_columns(ref, start):
    count = ref.shape[0]
    pieces = [ref[:, start : start + 8, PAD * g : PAD * g + PAD].reshape(8 * count, PAD) for g in range(4)]
    return jnp.concatenate(pieces, 0)


def unpack_points(ref):
    count = ref.shape[0]
    pieces = []
    for g in range(4):
        top, left = 8 * (g // 2), FEAT * (g % 2)
        pieces.append(ref[:, top : top + 8, left : left + FEAT].reshape(8 * count, FEAT))
    return jnp.concatenate(pieces, 0)


def places(rows=PAD, columns=PAD):
    shape = (rows, columns)
    return lax.broadcasted_iota(jnp.int32, shape, 0), lax.broadcasted_iota(jnp.int32, shape, 1)


def symmetric(matrix):
    return 0.5 * (matrix + matrix.T)


def join_symmetric(first, second):
    down, across = places()
    diagonal = jnp.sum(jnp.where(down == across, second, 0.0), 0, keepdims=True)
    return jnp.where(down == PAD - 1, diagonal, jnp.where(down >= across, first, second))


def part_symmetric(joined):
    down, across = places()
    inside = down < PAD - 1
    lower = jnp.where((down >= across) & inside, joined, 0.0)
    upper = jnp.where(down < across, joined, 0.0)
    eye = down == across
    first = jnp.where(eye, lower, lower + lower.T)
    second = upper + upper.T + jnp.where(eye, joined[PAD - 1 : PAD, :], 0.0)
    return first, second


def eliminate(systems):
    down, across = places(PAD, 2 * PAD)
    systems = [jnp.where((down == PAD - 1) & (across == PAD - 1), 1.0, system) for system in systems]
    for k in range(0, PAD, 2):
        first, second = down == k, down == k + 1
        for n, system in enumerate(systems):
            top, bottom = system[k : k + 1, :], system[k + 1 : k + 2, :]
            left, right = system[:, k : k + 1], system[:, k + 1 : k + 2]
            one, off, two = left[k : k + 1], right[k : k + 1], right[k + 1 : k + 2]
            scale = 1.0 / (one * two - off * off)
            upper = (two * top - off * bottom) * scale
            lower = (one * bottom - off * top) * scale
            rest = system - left * upper - right * lower
            systems[n] = jnp.where(first, upper, jnp.where(second, lower, rest))
    return [system[:, PAD:] for system in systems]


def identity():
    down, across = places()
    return jnp.where(down == across, 1.0, 0.0)


def pieces_of(array, count=3):
    pieces = []
    for _ in range(count):
        piece = array.astype(bf16)
        pieces.append(piece)
        array = array - piece.astype(f32)
    return pieces


def bdot(left, right, right_dim=0):
    return lax.dot_general(left, right, (((1,), (right_dim,)), ((), ())), preferred_element_type=f32)


def left_pieces(array):
    high, mid, low = pieces_of(array)
    return jnp.concatenate([high, high, high, mid, mid, low], 1)


def right_pieces(array, dim):
    high, mid, low = pieces_of(array)
    return jnp.concatenate([high, mid, low, high, mid, high], dim)


def wide_dot(left, right, right_dim=0):
    return bdot(left_pieces(left), right_pieces(right, right_dim), right_dim)


def tile_dot(tile_ref, right):
    first, second, third = pieces_of(right)
    both = jnp.concatenate([first, second], 1)
    by_high = bdot(tile_ref[0], jnp.concatenate([both, third], 1))
    by_mid = bdot(tile_ref[1], both)
    by_low = bdot(tile_ref[2], first)
    small = by_high[:, 2 * PAD :] + by_mid[:, PAD:] + by_low
    return by_high[:, :PAD] + (by_high[:, PAD : 2 * PAD] + by_mid[:, :PAD] + small)


def start_kernel(
    points_hbm, probes_hbm, targets_hbm, lengths_hbm, variances_hbm,
    own_ref, col_ref,
    points_ref, probes_ref, targets_ref, lengths_ref, variances_ref, sems,
):
    sources = (points_hbm, probes_hbm, targets_hbm, lengths_hbm, variances_hbm)
    targets = (points_ref, probes_ref, targets_ref, lengths_ref, variances_ref)
    copies = [pltpu.make_async_copy(a, b, sems.at[n]) for n, (a, b) in enumerate(zip(sources, targets))]
    for copy in copies:
        copy.start()
    for copy in copies:
        copy.wait()
    scaled = points_ref[...] / lengths_ref[...]
    rhs = jnp.concatenate([probes_ref[...], targets_ref[...], jnp.zeros((1, PAD), f32)], 0).T
    pairs = [jnp.concatenate([scaled[16 * g : 16 * g + 8], scaled[16 * g + 8 : 16 * g + 16]], 1) for g in range(2)]
    block = jnp.concatenate(pairs + [pack(rhs)], 0)
    scalars = jnp.concatenate([variances_ref[...], jnp.zeros((1, 126), f32)], 1)
    own_ref[...] = jnp.concatenate([block, jnp.broadcast_to(scalars, (8, 128))], 0)
    col_ref[...] = jnp.broadcast_to(block[None], col_ref.shape)


def variances_of(own_ref):
    return own_ref[8:9, 0:1], own_ref[8:9, 1:2]


def norm_lanes(points, first):
    squares = jnp.concatenate(pieces_of(points * points), 1)
    norms = bdot(squares, jnp.ones((squares.shape[1], 128), bf16))
    across = lax.broadcasted_iota(jnp.int32, norms.shape, 1)
    lanes = jnp.where((across >= 3 - first) & (across < 6 - first), 1.0, 0.0)
    for n, piece in enumerate(pieces_of(norms)):
        lanes = jnp.where(across == first + n, piece.astype(f32), lanes)
    return lanes.astype(bf16)


def tile_kernel(row_ref, col_ref, tile_hbm, message_ref, own_ref, work_ref, tile_ref, sems):
    own_ref[...] = row_ref[lax.axis_index("col"), 16:32, :]
    row_points = unpack_points(row_ref) * root_five
    col_points = unpack_points(col_ref) * root_five
    left = jnp.concatenate([left_pieces(row_points), norm_lanes(row_points, 0)], 1)
    right = jnp.concatenate([right_pieces(-2.0 * col_points, 1), norm_lanes(col_points, 3)], 1)
    work_ref[...] = bdot(left, right, 1)

    def strip(i, carry):
        here = pl.ds(pl.multiple_of(i * 16, 16), 16)
        squared = jnp.maximum(work_ref[here, :], 0.0)
        dist = squared * lax.rsqrt(jnp.maximum(squared, 1e-30))
        decayed = jnp.exp(-dist)
        more = 1.0 + dist
        pieces = pieces_of((more + squared * (1.0 / 3.0)) * decayed) + pieces_of(more * decayed, 2)
        for n, piece in enumerate(pieces):
            tile_ref[n, here, :] = piece
        return carry

    rows = work_ref.shape[0]
    part = rows // PARTS
    copies = []
    for n in range(PARTS):
        lax.fori_loop(n * (part // 16), (n + 1) * (part // 16), strip, 0)
        here = pl.ds(n * part, part)
        copies.append(pltpu.make_async_copy(tile_ref.at[:, here, :], tile_hbm.at[:, here, :], sems.at[n]))
        copies[n].start()
    row_rhs = unpack_columns(row_ref, 16)
    col_rhs = unpack_columns(col_ref, 16)
    own_rhs = unpack(own_ref[0:8, :])
    partial = tile_dot(tile_ref, col_rhs)
    curvature = dot(row_rhs, partial, 0, 0)
    gram = dot(own_rhs, own_rhs, 0, 0)
    quarter = rows // 4
    chunks = jnp.concatenate([partial[quarter * g : quarter * g + quarter] for g in range(4)], 1)
    message_ref[:, 0:8, :] = chunks.reshape(quarter // 8, 8, 128)
    grams = pack(join_symmetric(symmetric(curvature), gram))
    message_ref[:, 8:16, :] = jnp.broadcast_to(grams[None], (quarter // 8, 8, 128))
    for copy in copies:
        copy.wait()


def images_kernel(got_ref, own_ref, own_images_ref, col_ref):
    signal_var, noise_var = variances_of(own_ref)
    summed = jnp.sum(got_ref[...], 0)
    images = signal_var * summed[0:8] + noise_var * own_ref[0:8, :]
    own_images_ref[...] = images
    col_ref[...] = jnp.broadcast_to(jnp.concatenate([images, summed[8:16]], 0)[None], col_ref.shape)


def residual_of(rhs, images, advance):
    wide = jnp.concatenate([advance] * 4, 1)
    down, across = places(4 * PAD, 4 * PAD)
    repeated = jnp.where(down // PAD == across // PAD, jnp.concatenate([wide] * 4, 0), 0.0)
    return rhs - wide_dot(images, repeated)


def unpack_values(values):
    return jnp.concatenate([values[:, PAD * g : PAD * g + PAD] for g in range(4)], 0)


def packed_rows(ref, start):
    return ref[:, start : start + 8, :].reshape(8 * ref.shape[0], 128)


def grams_kernel(
    col_images_ref, row_images_ref, col_ref, row_ref, own_ref, own_images_ref, tile_hbm, coef_ref, message_ref, tile_ref, sems
):
    copy = pltpu.make_async_copy(tile_hbm.at[0:3], tile_ref, sems.at[0])
    copy.start()
    signal_var, noise_var = variances_of(own_ref)
    base_curvature, res_gram = part_symmetric(unpack(jnp.sum(col_images_ref[:, 8:16, :], 0)))
    curvature = signal_var * base_curvature + noise_var * res_gram
    (advance,) = eliminate([jnp.concatenate([curvature, res_gram], 1)])
    coef_ref[...] = jnp.concatenate([advance, res_gram, curvature, jnp.zeros((PAD, PAD), f32)], 1)
    col_res = unpack_values(residual_of(packed_rows(col_ref, 16), packed_rows(col_images_ref, 0), advance))
    row_res = unpack_values(residual_of(packed_rows(row_ref, 16), packed_rows(row_images_ref, 0), advance))
    own_res = unpack(residual_of(own_ref[0:8, :], own_images_ref[...], advance))
    copy.wait()
    product = tile_dot(tile_ref, col_res)
    next_curvature = dot(row_res, product, 0, 0)
    next_gram = dot(own_res, own_res, 0, 0)
    message = pack(join_symmetric(symmetric(next_curvature), next_gram))
    message_ref[...] = jnp.broadcast_to(message[None], message_ref.shape)


def prepare_kernel(
    coef_ref, row_ref, col_ref, row_images_ref, col_images_ref, left_ref, right_ref, points_ref, moments_ref, out_ref
):
    advance, res_gram, curvature = (coef_ref[:, PAD * g : PAD * g + PAD] for g in range(3))
    (inverse,) = eliminate([jnp.concatenate([res_gram, identity()], 1)])
    middle = dot(inverse, dot(curvature, inverse))
    out_ref[...] = jnp.concatenate([advance, inverse, symmetric(middle), jnp.zeros((PAD, PAD), f32)], 1)
    left_ref[...] = left_pieces(jnp.concatenate([unpack_columns(row_ref, 16), unpack_columns(row_images_ref, 0)], 1))
    right = jnp.concatenate([unpack_columns(col_ref, 16), unpack_columns(col_images_ref, 0)], 1)
    right_ref[...] = right_pieces(right, 1)
    points_ref[...] = unpack_points(row_ref)
    col_points = unpack_points(col_ref)
    moments = pieces_of(jnp.concatenate([col_points, col_points * col_points], 1), 2)
    moments_ref[...] = jnp.concatenate(moments, 1)


def spread_kernel(got_ref, out_ref):
    out_ref[...] = jnp.broadcast_to(jnp.sum(got_ref[...], 0)[None], out_ref.shape)


def gradient_kernel(
    total_points,
    got_ref,
    coef_ref,
    own_ref,
    own_images_ref,
    left_ref,
    right_ref,
    points_ref,
    moments_ref,
    tile_hbm,
    solves_ref,
    terms_ref,
    tile_ref,
    matrix_ref,
    weighted_ref,
    sums_ref,
    sems,
):
    copies = []
    for n, k in enumerate((0, 1, 3, 4)):
        copies.append(pltpu.make_async_copy(tile_hbm.at[k], tile_ref.at[n], sems.at[n]))
        copies[n].start()
    signal_var, noise_var = variances_of(own_ref)
    advance, inverse, middle = (coef_ref[:, PAD * g : PAD * g + PAD] for g in range(3))
    base_curvature, next_gram = part_symmetric(unpack(jnp.sum(got_ref[...], 0)))
    next_curv = signal_var * base_curvature + noise_var * next_gram - dot(dot(next_gram, middle), next_gram)
    carry_over = dot(inverse, next_gram)
    (next_advance,) = eliminate([jnp.concatenate([next_curv, next_gram], 1)])
    coef = wide_dot(jnp.concatenate([identity() + carry_over, -advance], 0), next_advance)
    coef = coef + jnp.concatenate([advance, jnp.zeros((PAD, PAD), f32)], 0)
    _, across = places(2 * PAD, PAD)
    weights = jnp.where(across < PROBES, -1.0 / PROBES, 1.0) * (0.5 / total_points)
    target = jnp.where(across == PROBES, coef, 0.0)
    form = dot(target * (0.5 / total_points), target, 1, 1)
    probes = jnp.where(across < PROBES, coef * weights, 0.0)
    form = form + jnp.concatenate([probes, jnp.zeros((2 * PAD, PAD), f32)], 1)
    left = bdot(left_ref[...], right_pieces(form, 0))
    matrix_ref[...] = bdot(left_pieces(left), right_ref[...], 1)

    own_rhs = unpack(own_ref[0:8, :])
    own_solves = dot(jnp.concatenate([own_rhs, unpack(own_images_ref[...])], 1), coef)
    solves_ref[...] = own_solves.T[0:COLS, :]
    pair = jnp.where(across[:PAD] < PROBES, own_rhs, own_solves)
    noise = jnp.sum(own_solves * weights[:PAD] * pair, 0, keepdims=True)
    noise_term = noise_var * jnp.sum(noise, 1, keepdims=True)
    for copy in copies:
        copy.wait()

    def strip(i, total):
        here = pl.ds(pl.multiple_of(i * 16, 16), 16)
        values = matrix_ref[here, :]
        high, mid, slope_high, slope_low = (tile_ref[n, here, :].astype(f32) for n in range(4))
        weighted = values * (slope_high + slope_low)
        upper = weighted.astype(bf16)
        weighted_ref[0, here, :] = upper
        weighted_ref[1, here, :] = (weighted - upper.astype(f32)).astype(bf16)
        sums_ref[here, :] = sum(weighted[:, 128 * g : 128 * g + 128] for g in range(weighted.shape[1] // 128))
        return total + values * (high + mid)

    signal = lax.fori_loop(0, matrix_ref.shape[0] // 16, strip, jnp.zeros((16, matrix_ref.shape[1]), f32))
    by_upper = bdot(weighted_ref[0], moments_ref[...])
    moved = by_upper[:, :128] + (by_upper[:, 128:] + bdot(weighted_ref[1], moments_ref[:, :128]))
    sums_high, sums_low = pieces_of(sums_ref[...], 2)
    ones = jnp.ones((128, 128), bf16)
    row_sums = bdot(sums_high, ones) + bdot(sums_low, ones)
    points = points_ref[...]
    scales = points * (points * row_sums[:, :FEAT] - 2.0 * moved[:, :FEAT]) + moved[:, FEAT:128]
    scale_terms = (5.0 / 3.0 * signal_var) * jnp.sum(scales, 0, keepdims=True)
    signal_term = signal_var * jnp.sum(jnp.sum(signal, 0, keepdims=True), 1, keepdims=True)
    terms_ref[...] = jnp.concatenate([scale_terms, signal_term, noise_term, jnp.zeros((1, FEAT - 2), f32)], 1)


def shape_of(*dims, dtype=f32):
    return jax.ShapeDtypeStruct(dims, dtype)


def call(kernel, outs, *operands, far_in=0, far_outs=0, scratch=(), limit=NEAR):
    near, far = (pl.BlockSpec(memory_space=m) for m in (pltpu.VMEM, pltpu.HBM))
    return pl.pallas_call(
        kernel,
        out_shape=outs,
        in_specs=[near] * (len(operands) - far_in) + [far] * far_in,
        out_specs=[far] * far_outs + [near] * (len(outs) - far_outs),
        scratch_shapes=scratch,
        compiler_params=pltpu.CompilerParams(vmem_limit_bytes=limit),
        cost_estimate=pl.CostEstimate(flops=1, bytes_accessed=1 << 20, transcendentals=0),
    )(*operands)


def exchange(blocks, axis):
    return lax.all_to_all(blocks, axis, 0, 0, tiled=True)


def local(points, length_scales, variances, targets, probe_vectors):
    rows = lax.axis_size("row")
    cols = lax.axis_size("col")
    width = points.shape[1]
    row_block, col_set = cols * width, rows * width
    total_points = width * rows * cols
    tile = (row_block, col_set)
    sems = pltpu.SemaphoreType.DMA((4,))

    to_row, to_col = call(
        start_kernel,
        [shape_of(32, 128), shape_of(rows, 24, 128)],
        points.T,
        probe_vectors,
        targets[None],
        length_scales[None],
        variances[None],
        far_in=5,
        limit=WHOLE,
        scratch=[
            pltpu.VMEM((width, FEAT), f32),
            pltpu.VMEM((PROBES, width), f32),
            pltpu.VMEM((1, width), f32),
            pltpu.VMEM((1, FEAT), f32),
            pltpu.VMEM((1, 2), f32),
            pltpu.SemaphoreType.DMA((5,)),
        ],
    )
    col_got = exchange(to_col, "row")
    row_got = lax.all_gather(to_row, "col")
    stack, message, own = call(
        tile_kernel,
        [shape_of(5, *tile, dtype=bf16), shape_of(cols, 16, 128), shape_of(16, 128)],
        row_got,
        col_got,
        far_outs=1,
        limit=LARGE,
        scratch=[pltpu.VMEM(tile, f32), pltpu.VMEM((5,) + tile, bf16), sems],
    )
    own_images, images_col = call(
        images_kernel, [shape_of(8, 128), shape_of(rows, 16, 128)], exchange(message, "col"), own
    )
    col_images = exchange(images_col, "row")
    row_images = lax.all_gather(own_images, "col")
    coef, message = call(
        grams_kernel,
        [shape_of(PAD, 128), shape_of(cols, 8, 128)],
        col_images,
        row_images,
        col_got,
        row_got,
        own,
        own_images,
        stack,
        far_in=1,
        limit=LARGE,
        scratch=[pltpu.VMEM((3,) + tile, bf16), sems],
    )
    *prepared, coef = call(
        prepare_kernel,
        [
            shape_of(row_block, 12 * PAD, dtype=bf16),
            shape_of(col_set, 12 * PAD, dtype=bf16),
            shape_of(row_block, FEAT),
            shape_of(col_set, 4 * FEAT, dtype=bf16),
            shape_of(PAD, 128),
        ],
        coef,
        row_got,
        col_got,
        row_images,
        col_images,
    )
    (message,) = call(spread_kernel, [shape_of(rows, 8, 128)], exchange(message, "col"))
    solves, terms = call(
        functools.partial(gradient_kernel, total_points),
        [shape_of(COLS, width), shape_of(1, 128)],
        exchange(message, "row"),
        coef,
        own,
        own_images,
        *prepared,
        stack,
        far_in=1,
        limit=LARGE,
        scratch=[
            pltpu.VMEM((4,) + tile, bf16),
            pltpu.VMEM(tile, f32),
            pltpu.VMEM((2,) + tile, bf16),
            pltpu.VMEM((row_block, 128), f32),
            sems,
        ],
    )
    terms = jnp.sum(exchange(jnp.broadcast_to(terms[None], (cols, 1, 128)), "col"), 0)
    terms = exchange(jnp.broadcast_to(terms[None], (rows, 1, 128)), "row")
    return (solves, jnp.sum(terms[:, 0, : FEAT + 2], 0))


def solution(mesh):
    placed = (P(None, ("row", "col")), P(), P(), P(("row", "col")), P(None, ("row", "col")))
    return jax.shard_map(
        local, mesh=mesh, in_specs=placed, out_specs=(P(None, ("row", "col")), P()), check_vma=False
    )
```
